512 devices in a mesh: bucket: 16 (over x_lo, y), edge: 32 (over x_hi, z, core).
Axes of the slice: x: 4 (x_hi: 2, x_lo: 2; x = x_hi * 2 + x_lo), y: 8, z: 8, core: 2. Of those that a mesh axis runs over, the one named last changes fastest.
Arguments:
- entity_block: float32 [4096, 400], P('bucket'), may hold values from -1.25 to 1.25
- block_state: float32 [4096], P('bucket'), may hold values from 50 to 5000
- hot_entities: float32 [512, 400], replicated, may hold values from -1.25 to 1.25
- hot_state: float32 [512], replicated, may hold values from 0.05 to 1
- relations: float32 [8192, 400], P('edge'), may hold values from -6 to 6
- relation_state: float32 [8192], P('edge'), may hold values from 4 to 400
- source_ids: int32 [16, 20480], P('bucket', 'edge'), may hold values from 0 to 767
- target_ids: int32 [16, 20480], P('bucket', 'edge'), may hold values from 0 to 767
- relation_ids: int32 [16, 20480], P('bucket', 'edge'), may hold values from 0 to 255
- negative_ids: int32 [16, 32, 1000], P('bucket', 'edge'), may hold values from 0 to 255
Outputs:
- new_block: float32 [4096, 400], P('bucket')
- new_block_state: float32 [4096], P('bucket')
- new_hot: float32 [512, 400], replicated
- new_hot_state: float32 [512], replicated
- new_relations: float32 [8192, 400], P('edge')
- new_relation_state: float32 [8192], P('edge')
The draws below stay inside these ranges and needn't reach their ends.
Inputs may be any that keep to these rules, and one draw needn't show every extreme that they name: `source_ids`: ids below 256 name cold rows of a partition block, the others hot row id - 256. `target_ids`: ids below 256 name cold rows of the partner's block, the others hot row id - 256. `negative_ids`: rows of the partner's block.
All inputs are finite; a program needn't handle non-finite values.
Results may differ from the reference program's by a relative error of at most 0.0081.
Values may be sent and summed in bfloat16 or wider, within the bound.
No kernel may reach another device: no remote copies, remote signals or barrier semaphores. Data moves between devices by JAX's collectives and lax.ppermute only.
A program may use at most 64 MiB of HBM per device.

```python
import math
import jax
import jax.numpy as jnp
import numpy as np
from jax import lax

D = 400
NEG = 1000
GROUPS_DEV = 1
ROWS_DEV = 256
HOT = 512
REL_DEV = 256
RELATIONS = 8192
BUCKETS = 16
EDGES_DEV = 640
N_BUCKET = 16
N_EDGE = 32


def place_ends(drawn, key, smallest, high):
    place = [jax.random.randint(jax.random.fold_in(key, axis), (), 0, length) for axis, length in enumerate(drawn.shape)]
    widest = drawn.shape.index(max(drawn.shape))
    neighbour = place[:widest] + [(place[widest] + 1) % drawn.shape[widest]] + place[widest + 1:]
    return drawn.at[tuple(place)].set(smallest).at[tuple(neighbour)].set(high)


def block_scale(stream_key, extent, shards, low, largest):
    level, own = 1.0, jax.random.fold_in(stream_key, 6)
    for axis_at, shards_of in shards:
        heights = jnp.exp(jax.random.uniform(jax.random.fold_in(own, axis_at), (shards_of,), jnp.float32, low / len(shards), largest / len(shards)))
        level = level * jnp.repeat(heights, extent[axis_at] // shards_of).reshape([-1 if axis == axis_at else 1 for axis in range(len(extent))])
    return level


def rank_bounds(number_of, slope):
    loads = [(1 << 20) // math.isqrt(standing ** slope) + 1 for standing in range(1, number_of + 1)]
    deviation = 1 + sum(loads) // (1 << 30)
    return np.cumsum(np.array([max(1, weight // deviation) for weight in loads]))


def skewed_ids(rng, dims, amount, slope):
    grid = rank_bounds(amount, slope)
    ticket = jax.random.randint(jax.random.fold_in(rng, 1), dims, 0, int(grid[amount - 1]))
    rank = jnp.searchsorted(jnp.asarray(grid, jnp.int32), ticket, side="right")
    return jax.random.permutation(jax.random.fold_in(rng, 2), amount)[rank].astype(jnp.int32)


def normal_values(stream_key, shape, spread, reach, split=(), kind=jnp.bfloat16):
    factor_of = block_scale(stream_key, shape, split, -0.22, 0.18) if split else 1.0
    entries = jax.random.normal(stream_key, shape, jnp.float32) * spread * factor_of
    return jnp.minimum(jnp.maximum(entries, -reach), reach).astype(kind)


def setup_inputs(seed: int = 0) -> dict:
    arg_keys = jax.random.split(jax.random.key(seed), 11)
    return {
        "entity_block": normal_values(arg_keys[0], (BUCKETS * ROWS_DEV, D), 0.22, 1.25, ((0, 16),), jnp.float32),
        "block_state": jnp.clip(jnp.exp(math.log(5000.0) - 4.6051702 * jax.random.uniform(arg_keys[1], (BUCKETS * ROWS_DEV,), jnp.float32) ** block_scale(arg_keys[1], (BUCKETS * ROWS_DEV,), ((0, 16),), -0.2, 0.2)), 50.0, 5000.0),
        "hot_entities": normal_values(arg_keys[2], (HOT, D), 0.22, 1.25, (), jnp.float32),
        "hot_state": jnp.clip(jnp.exp(jax.random.uniform(arg_keys[3], (HOT,), jnp.float32, math.log(0.05), math.log(1.0))), 0.05, 1.0),
        "relations": normal_values(arg_keys[4], (RELATIONS, D), 1.0, 6.0, ((0, 32),), jnp.float32),
        "relation_state": jnp.clip(jnp.exp(math.log(400.0) - 4.6051702 * jax.random.uniform(arg_keys[5], (RELATIONS,), jnp.float32) ** block_scale(arg_keys[5], (RELATIONS,), ((0, 32),), -0.2, 0.2)), 4.0, 400.0),
        "source_ids": place_ends(skewed_ids(arg_keys[6], (BUCKETS, N_EDGE * EDGES_DEV), ROWS_DEV + HOT, 2), jax.random.fold_in(arg_keys[6], 3), 0, (ROWS_DEV + HOT) - 1).astype(jnp.int32),
        "target_ids": place_ends(skewed_ids(arg_keys[7], (BUCKETS, N_EDGE * EDGES_DEV), ROWS_DEV + HOT, 2), jax.random.fold_in(arg_keys[7], 3), 0, (ROWS_DEV + HOT) - 1).astype(jnp.int32),
        "relation_ids": place_ends(skewed_ids(arg_keys[8], (BUCKETS, N_EDGE * EDGES_DEV), REL_DEV, 1), jax.random.fold_in(arg_keys[8], 3), 0, REL_DEV - 1).astype(jnp.int32),
        "negative_ids": place_ends(jax.random.randint(arg_keys[9], (BUCKETS, N_EDGE * GROUPS_DEV, NEG), 0, ROWS_DEV), jax.random.fold_in(arg_keys[9], 1), 0, ROWS_DEV - 1).astype(jnp.int32),
    }


STEP = 0.3
EPS = 1e-06

def adagrad(weights, state_rows, grads):
    new_state = state_rows + lax.optimization_barrier(jnp.mean(grads * grads, axis=-1))
    return (weights - STEP * grads / (jnp.sqrt(new_state)[:, None] + EPS), new_state)

def device_grads(own_table, partner_table, hot_table, kind_table, sources, targets, kinds, negatives):
    rows = own_table.shape[0]
    hot_rows = hot_table.shape[0]
    width = own_table.shape[1]
    src_rows = jnp.concatenate([own_table, hot_table], axis=0)[sources]
    dst_rows = jnp.concatenate([partner_table, hot_table], axis=0)[targets]
    rel_rows = kind_table[kinds]
    queries = (src_rows.astype(jnp.float32) * rel_rows.astype(jnp.float32)).astype(jnp.bfloat16)
    positive = lax.optimization_barrier(jnp.sum(queries.astype(jnp.float32) * dst_rows.astype(jnp.float32), axis=-1))
    pos_grad = -jax.nn.sigmoid(-positive)
    groups = negatives.shape[0]
    blocked = queries.reshape(groups, -1, width).astype(jnp.float32)
    neg_rows = partner_table[negatives].astype(jnp.float32)
    scores = jnp.einsum('cqd,cnd->cqn', blocked, neg_rows)
    neg_grad = jax.nn.sigmoid(scores).astype(jnp.bfloat16).astype(jnp.float32)
    query_grad = pos_grad[:, None] * dst_rows.astype(jnp.float32) + jnp.einsum('cqn,cnd->cqd', neg_grad, neg_rows).reshape(-1, width)
    row_grad = jnp.einsum('cqn,cqd->cnd', neg_grad, blocked)
    src_grad = query_grad * rel_rows.astype(jnp.float32)
    kind_grad = query_grad * src_rows.astype(jnp.float32)
    dst_grad = pos_grad[:, None] * queries.astype(jnp.float32)
    src_sum = jax.ops.segment_sum(src_grad, sources, rows + hot_rows)
    dst_sum = jax.ops.segment_sum(dst_grad, targets, rows + hot_rows)
    neg_sum = jax.ops.segment_sum(row_grad.reshape(-1, width), negatives.reshape(-1), rows)
    kind_sum = jax.ops.segment_sum(kind_grad, kinds, kind_table.shape[0])
    return (src_sum[:rows], dst_sum[:rows] + neg_sum, src_sum[rows:] + dst_sum[rows:], kind_sum)

def reference(entity_block, block_state, hot_entities, hot_state, relations, relation_state, source_ids, target_ids, relation_ids, negative_ids):
    blocks = entity_block.astype(jnp.bfloat16).reshape(N_BUCKET, ROWS_DEV, D)
    hot_table = hot_entities.astype(jnp.bfloat16)
    kind_tables = relations.astype(jnp.bfloat16).reshape(N_EDGE, REL_DEV, D)
    sources = source_ids.reshape(N_BUCKET, N_EDGE, EDGES_DEV)
    targets = target_ids.reshape(N_BUCKET, N_EDGE, EDGES_DEV)
    kinds = relation_ids.reshape(N_BUCKET, N_EDGE, EDGES_DEV)
    negatives = negative_ids.reshape(N_BUCKET, N_EDGE, GROUPS_DEV, NEG)
    half_way = N_BUCKET // 2

    def step(carry, index):
        own_acc, partner_acc, hot_acc, kind_acc = carry
        bucket = (index // N_EDGE).astype(jnp.int32)
        edge_index = (index % N_EDGE).astype(jnp.int32)
        partner = jnp.bitwise_xor(bucket, jnp.int32(half_way))
        own_grad, partner_grad, hot_grad, kind_grad = device_grads(blocks[bucket], blocks[partner], hot_table, kind_tables[edge_index], sources[bucket, edge_index], targets[bucket, edge_index], kinds[bucket, edge_index], negatives[bucket, edge_index])
        own_acc = own_acc.at[bucket].add(own_grad)
        partner_acc = partner_acc.at[partner].add(partner_grad)
        kind_acc = kind_acc.at[edge_index].add(kind_grad)
        return ((own_acc, partner_acc, hot_acc + hot_grad, kind_acc), None)
    start = (jnp.zeros((N_BUCKET, ROWS_DEV, D), jnp.float32), jnp.zeros((N_BUCKET, ROWS_DEV, D), jnp.float32), jnp.zeros((HOT, D), jnp.float32), jnp.zeros((N_EDGE, REL_DEV, D), jnp.float32))
    totals, _ = lax.scan(step, start, jnp.arange(N_BUCKET * N_EDGE, dtype=jnp.int32))
    own_acc, partner_acc, hot_acc, kind_acc = totals
    block_grad = (own_acc + partner_acc).reshape(N_BUCKET * ROWS_DEV, D)
    new_block, new_block_state = adagrad(entity_block, block_state, block_grad)
    new_hot, new_hot_state = adagrad(hot_entities, hot_state, hot_acc)
    new_relations, new_relation_state = adagrad(relations, relation_state, kind_acc.reshape(N_EDGE * REL_DEV, D))
    return (new_block, new_block_state, new_hot, new_hot_state, new_relations, new_relation_state)
```

```python
import jax
import jax.numpy as jnp
from jax import lax
from jax.experimental import pallas as pl
from jax.experimental.pallas import tpu as pltpu
from jax.sharding import PartitionSpec as P

STEP = 0.3
EPS = 1e-06
F32 = jnp.float32
BF16 = jnp.bfloat16
PEERS = 16
VMEM = pl.BlockSpec(memory_space=pltpu.VMEM)


def call(body, outs, args, flops=1 << 22):
    moved = sum(a.size * a.dtype.itemsize for a in args)
    return pl.pallas_call(
        body,
        out_shape=[jax.ShapeDtypeStruct(shape, dtype) for shape, dtype in outs],
        in_specs=[VMEM] * len(args),
        out_specs=[VMEM] * len(outs),
        compiler_params=pltpu.CompilerParams(vmem_limit_bytes=40 << 20),
        cost_estimate=pl.CostEstimate(flops=flops, bytes_accessed=moved, transcendentals=0),
    )(*args)


def one_hot(ids, rows):
    grid = lax.broadcasted_iota(jnp.int32, (rows, ids.shape[1]), 0)
    return jnp.where(grid == ids, 1.0, 0.0).astype(BF16)


def mm(a, b):
    return lax.dot_general(a, b, (((1,), (0,)), ((), ())), preferred_element_type=F32)


def mm_t(a, b):
    return lax.dot_general(a, b, (((1,), (1,)), ((), ())), preferred_element_type=F32)


def core_of():
    return lax.axis_index("edge") & 1


def gather_kernel(own, hot, rel, src_ids, dst_ids, rel_ids, src_out, rel_out, dst_out):
    rows = own.shape[1]
    hot_rows = hot.shape[1]
    hot_bf = hot[...].astype(BF16)
    src_hot = one_hot(src_ids[...] - rows, hot_rows)
    src_own = one_hot(src_ids[...], rows)
    src_out[...] = (mm(own[...], src_own) + mm(hot_bf, src_hot)).astype(BF16)
    rel_out[...] = mm(rel[...].astype(BF16), one_hot(rel_ids[...], rel.shape[1])).astype(BF16)
    dst_out[...] = mm(hot_bf, one_hot(dst_ids[...] - rows, hot_rows)).astype(BF16)


def grad_kernel(
    partner, src, rel, dst_hot, src_ids, dst_ids, rel_ids, neg_ids, keep, send, kind
):
    width, rows = partner.shape
    hot_rows = 2 * rows
    core = core_of()
    src_f = src[...].astype(F32)
    rel_f = rel[...].astype(F32)
    query = (src_f * rel_f).astype(BF16)
    query_f = query.astype(F32)
    dst_own = one_hot(dst_ids[...], rows)
    dst = mm(partner[...], dst_own) + dst_hot[...].astype(F32)
    positive = jnp.sum(query_f * dst, axis=0, keepdims=True)
    pos_grad = -1.0 / (1.0 + jnp.exp(positive))
    scores = mm(partner[...].T, query)
    sig = (1.0 / (1.0 + jnp.exp(-scores))).astype(BF16)
    named = one_hot(neg_ids[...], rows)
    count = mm_t(jnp.ones((8, neg_ids.shape[1]), BF16), named)[:1, :]
    scaled = partner[...].astype(F32) * count
    high = scaled.astype(BF16)
    low = (scaled - high.astype(F32)).astype(BF16)
    query_grad = pos_grad * dst + mm(high, sig) + mm(low, sig)
    row_grad = mm_t(query, sig) * count
    src_grad = (query_grad * rel_f).astype(BF16)
    kind_grad = (query_grad * src_f).astype(BF16)
    dst_grad = (pos_grad * query_f).astype(BF16)
    kind[:width, :] = mm_t(kind_grad, one_hot(rel_ids[...], kind.shape[1])).astype(BF16)
    kind[width:, :] = jnp.zeros((kind.shape[0] - width, kind.shape[1]), BF16)
    half = rows // 2
    src_at = src_ids[...]
    dst_at = dst_ids[...]
    own_flip = core * half
    hot_flip = core * rows
    own_src = mm_t(src_grad, one_hot(jnp.where(src_at < rows, src_at ^ own_flip, -1), rows))
    hot_sum = mm_t(
        src_grad, one_hot(jnp.where(src_at < rows, -1, (src_at - rows) ^ hot_flip), hot_rows)
    ) + mm_t(dst_grad, one_hot(jnp.where(dst_at < rows, -1, (dst_at - rows) ^ hot_flip), hot_rows))
    partner_dst = mm_t(dst_grad, one_hot(jnp.where(dst_at < rows, dst_at ^ own_flip, -1), rows))
    first = core == 0
    neg_keep = jnp.where(first, row_grad[:, :half], row_grad[:, half:])
    neg_send = jnp.where(first, row_grad[:, half:], row_grad[:, :half])
    keep[:, :half] = own_src[:, :half]
    keep[:, half : 2 * half] = partner_dst[:, :half] + neg_keep
    keep[:, 2 * half :] = hot_sum[:, :rows]
    send[:, :half] = own_src[:, half:].astype(BF16)
    send[:, half : 2 * half] = (partner_dst[:, half:] + neg_send).astype(BF16)
    send[:, 2 * half :] = hot_sum[:, rows:].astype(BF16)


def add_kernel(keep, got, out):
    width = keep.shape[0]
    out[:width, :] = (keep[...] + got[...].astype(F32)).astype(BF16)
    out[width:, :] = jnp.zeros((out.shape[0] - width, out.shape[1]), BF16)


def chunk_sum(ref, lanes):
    rows = ref.shape[0] // PEERS
    total = ref[:rows, lanes].astype(F32)
    for peer in range(1, PEERS):
        total = total + ref[peer * rows : (peer + 1) * rows, lanes].astype(F32)
    return total


def bucket_kernel(got, kind, out, own, partner):
    rows = got.shape[0] // PEERS
    lanes = kind.shape[1]
    half = lanes // 2
    own[...] = chunk_sum(got, slice(0, half))
    partner[...] = chunk_sum(got, slice(half, lanes))
    hot = chunk_sum(got, slice(lanes, 2 * lanes)).astype(BF16)
    out[:, :lanes] = kind[...]
    for peer in range(PEERS):
        out[peer * rows : (peer + 1) * rows, lanes:] = hot


def spread_kernel(got, own, partner, out, kind):
    rows = got.shape[0] // PEERS
    lanes = got.shape[1] // 2
    half = own.shape[1]
    kind_sum = chunk_sum(got, slice(0, lanes)).astype(BF16)
    hot_sum = chunk_sum(got, slice(lanes, 2 * lanes)).astype(BF16)
    own_sum = (own[...] + partner[...]).astype(BF16)
    for peer in range(PEERS):
        at = slice(peer * rows, (peer + 1) * rows)
        out[at, :half] = own_sum
        out[at, half:] = hot_sum
        kind[at, :] = kind_sum


def adagrad(weights, state, grads, new_weights, new_state, at):
    total = state[:, at] + jnp.sum(grads * grads, axis=0, keepdims=True) / grads.shape[0]
    new_state[:, at] = total
    new_weights[:, at] = weights[:, at] - grads * (STEP / (jnp.sqrt(total) + EPS))


def entity_kernel(mine, other, block, block_state, hot, hot_state, new_b, new_bs, new_h, new_hs):
    width, rows = block.shape
    half = rows // 2
    first = core_of() == 0
    for part in range(2):
        low = jnp.where(first, part == 0, part == 1)
        grads = jnp.where(low, mine[:width, :], other[:width, :]).astype(F32)
        adagrad(block, block_state, grads[:, :half], new_b, new_bs, slice(part * half, (part + 1) * half))
        adagrad(hot, hot_state, grads[:, half:], new_h, new_hs, slice(part * rows, (part + 1) * rows))


def relation_kernel(grads, weights, state, new_weights, new_state):
    width, rows = weights.shape
    adagrad(weights, state, grads[:width, :].astype(F32), new_weights, new_state, slice(0, rows))


def flipped(x, axis, bit):
    return lax.ppermute(x, axis, [(i, i ^ bit) for i in range(lax.axis_size(axis))])


def exchanged(x, axis, groups=None):
    return lax.all_to_all(x, axis, 0, 0, tiled=True, axis_index_groups=groups)


def local(
    entity_block,
    block_state,
    hot_entities,
    hot_state,
    relations,
    relation_state,
    source_ids,
    target_ids,
    relation_ids,
    negative_ids,
):
    rows, width = entity_block.shape
    hot_rows = hot_entities.shape[0]
    edges = source_ids.shape[1]
    padded = -(-width // 256) * 256
    slot = padded // PEERS
    half = rows // 2
    block_t, hot_t, rel_t = entity_block.T, hot_entities.T, relations.T
    negatives = negative_ids.reshape(1, -1)
    own_bf = block_t.astype(BF16)
    swap = lax.axis_size("bucket") // 2
    partner = flipped(own_bf, "bucket", swap)
    src, rel, dst_hot = call(
        gather_kernel,
        [((width, edges), BF16)] * 3,
        (own_bf, hot_t, rel_t, source_ids, target_ids, relation_ids),
        1 << 30,
    )
    keep, send, kind = call(
        grad_kernel,
        [((width, 2 * rows), F32), ((width, 2 * rows), BF16), ((padded, rows), BF16)],
        (partner, src, rel, dst_hot, source_ids, target_ids, relation_ids, negatives),
        1 << 31,
    )
    pairs = [[2 * i + core for i in range(PEERS)] for core in range(2)]
    (mixed,) = call(add_kernel, [((padded, 2 * rows), BF16)], (keep, flipped(send, "edge", 1)))
    mixed = exchanged(mixed, "edge", pairs)
    to_bucket, own_part, partner_part = call(
        bucket_kernel,
        [((padded, 2 * rows), BF16), ((slot, half), F32), ((slot, half), F32)],
        (mixed, kind),
    )
    returned = flipped(partner_part, "bucket", swap)
    from_bucket = exchanged(to_bucket, "bucket")
    entity_part, kind_part = call(
        spread_kernel,
        [((padded, half + rows), BF16), ((padded, rows), BF16)],
        (from_bucket, own_part, returned),
    )
    mine = exchanged(entity_part, "edge", pairs)
    mine, kind_part = lax.optimization_barrier((mine, kind_part))
    other = flipped(mine, "edge", 1)
    kind_grads = exchanged(kind_part, "bucket")
    new_block, new_block_state, new_hot, new_hot_state = call(
        entity_kernel,
        [((width, rows), F32), ((1, rows), F32), ((width, hot_rows), F32), ((1, hot_rows), F32)],
        (mine, other, block_t, block_state.reshape(1, -1), hot_t, hot_state.reshape(1, -1)),
    )
    new_relations, new_relation_state = call(
        relation_kernel,
        [((width, rows), F32), ((1, rows), F32)],
        (kind_grads, rel_t, relation_state.reshape(1, -1)),
    )
    return (
        new_block.T,
        new_block_state.reshape(-1),
        new_hot.T,
        new_hot_state.reshape(-1),
        new_relations.T,
        new_relation_state.reshape(-1),
    )


def solution(mesh):
    placed = (
        P("bucket", None),
        P("bucket"),
        P(),
        P(),
        P("edge", None),
        P("edge"),
        P("bucket", "edge"),
        P("bucket", "edge"),
        P("bucket", "edge"),
        P("bucket", "edge", None),
    )
    return jax.shard_map(
        local,
        mesh=mesh,
        in_specs=placed,
        out_specs=(P("bucket", None), P("bucket"), P(), P(), P("edge", None), P("edge")),
        check_vma=False,
    )
```

```python
import jax
import jax.numpy as jnp
from jax import lax
from jax.experimental import pallas as pl
from jax.experimental.pallas import tpu as pltpu
from jax.sharding import PartitionSpec as P

STEP = 0.3
EPS = 1e-06
F32 = jnp.float32
BF16 = jnp.bfloat16
PEERS = 16
VMEM = pl.BlockSpec(memory_space=pltpu.VMEM)


def call(body, outs, args, flops=1 << 22):
    moved = sum(a.size * a.dtype.itemsize for a in args)
    return pl.pallas_call(
        body,
        out_shape=[jax.ShapeDtypeStruct(shape, dtype) for shape, dtype in outs],
        in_specs=[VMEM] * len(args),
        out_specs=[VMEM] * len(outs),
        compiler_params=pltpu.CompilerParams(vmem_limit_bytes=40 << 20),
        cost_estimate=pl.CostEstimate(flops=flops, bytes_accessed=moved, transcendentals=0),
    )(*args)


def one_hot(ids, rows):
    grid = lax.broadcasted_iota(jnp.int32, (rows, ids.shape[1]), 0)
    return jnp.where(grid == ids, 1.0, 0.0).astype(BF16)


def mm(a, b):
    return lax.dot_general(a, b, (((1,), (0,)), ((), ())), preferred_element_type=F32)


def mm_t(a, b):
    return lax.dot_general(a, b, (((1,), (1,)), ((), ())), preferred_element_type=F32)


def core_of():
    return lax.axis_index("edge") & 1


def pack_kernel(block, src_ids, dst_ids, rel_ids, neg_ids, table, ids):
    table[...] = block[...].astype(BF16)
    ids[...] = jnp.full(ids.shape, -1, jnp.int32)
    for row, part in enumerate((src_ids, dst_ids, rel_ids, neg_ids)):
        ids[row : row + 1, : part.shape[1]] = part[...]


def id_rows(ids, edges):
    return ids[0:1, :edges], ids[1:2, :edges], ids[2:3, :edges], ids[3:4, :]


def gather_kernel(own, hot, rel, ids, src_out, rel_out, dst_out, hot_bf, rel_bf):
    rows = own.shape[1]
    hot_rows = hot.shape[1]
    src_at, dst_at, rel_at, _ = id_rows(ids, src_out.shape[1])
    hot_bf[...] = hot[...].astype(BF16)
    rel_bf[...] = rel[...].astype(BF16)
    src_out[...] = (
        mm(own[...], one_hot(src_at, rows)) + mm(hot_bf[...], one_hot(src_at - rows, hot_rows))
    ).astype(BF16)
    rel_out[...] = mm(rel_bf[...], one_hot(rel_at, rel.shape[1])).astype(BF16)
    dst_out[...] = mm(hot_bf[...], one_hot(dst_at - rows, hot_rows)).astype(BF16)


def edge_grads(partner, src, rel, dst, neg_at):
    query = (src * rel).astype(BF16)
    query_f = query.astype(F32)
    positive = jnp.sum(query_f * dst, axis=0, keepdims=True)
    pos_grad = -1.0 / (1.0 + jnp.exp(positive))
    scores = mm(partner.T, query)
    sig = (1.0 / (1.0 + jnp.exp(-scores))).astype(BF16)
    named = one_hot(neg_at, partner.shape[1])
    count = mm_t(jnp.ones((8, neg_at.shape[1]), BF16), named)[:1, :]
    scaled = partner.astype(F32) * count
    high = scaled.astype(BF16)
    low = (scaled - high.astype(F32)).astype(BF16)
    query_grad = pos_grad * dst + mm(high, sig) + mm(low, sig)
    src_grad = (query_grad * rel).astype(BF16)
    kind_grad = (query_grad * src).astype(BF16)
    dst_grad = (pos_grad * query_f).astype(BF16)
    return query, sig, count, src_grad, kind_grad, dst_grad


def grad_kernel(own, partner, hot, rel, src, rel_rows, dst_hot, ids, far_ids, keep, send, kind):
    width, rows = own.shape
    hot_rows = hot.shape[1]
    half = rows // 2
    edges = src.shape[1]
    core = core_of()
    side = lax.axis_index("bucket") // (lax.axis_size("bucket") // 2)
    own_flip = core * half

    def hot_at(at):
        local_at = at - rows - side * (hot_rows // 2)
        inside = (local_at >= 0) & (local_at < hot_rows // 2)
        return jnp.where(inside, local_at ^ own_flip, -1)

    def cold_at(at):
        return jnp.where(at < rows, at ^ own_flip, -1)

    src_at, dst_at, rel_at, neg_at = id_rows(ids, edges)
    dst = mm(partner[...], one_hot(dst_at, rows)) + dst_hot[...].astype(F32)
    _, _, _, src_grad, kind_grad, dst_grad = edge_grads(
        partner[...], src[...].astype(F32), rel_rows[...].astype(F32), dst, neg_at
    )
    block_sum = mm_t(src_grad, one_hot(cold_at(src_at), rows))
    hot_sum = mm_t(src_grad, one_hot(hot_at(src_at), rows))
    hot_sum += mm_t(dst_grad, one_hot(hot_at(dst_at), rows))
    kind_sum = mm_t(kind_grad, one_hot(rel_at - side * half, half))

    src_at, dst_at, rel_at, neg_at = id_rows(far_ids, edges)
    far_src = mm(partner[...], one_hot(src_at, rows)) + mm(hot[...], one_hot(src_at - rows, hot_rows))
    far_dst = mm(own[...], one_hot(dst_at, rows)) + mm(hot[...], one_hot(dst_at - rows, hot_rows))
    far_rel = mm(rel[...], one_hot(rel_at, rel.shape[1]))
    query, sig, count, src_grad, kind_grad, dst_grad = edge_grads(
        own[...], far_src, far_rel, far_dst, neg_at
    )
    row_grad = mm_t(query, sig) * count
    block_sum += mm_t(dst_grad, one_hot(cold_at(dst_at), rows))
    hot_sum += mm_t(src_grad, one_hot(hot_at(src_at), rows))
    hot_sum += mm_t(dst_grad, one_hot(hot_at(dst_at), rows))
    kind_sum += mm_t(kind_grad, one_hot(rel_at - side * half, half))

    first = core == 0
    neg_keep = jnp.where(first, row_grad[:, :half], row_grad[:, half:])
    neg_send = jnp.where(first, row_grad[:, half:], row_grad[:, :half])
    keep[:, :half] = block_sum[:, :half] + neg_keep
    keep[:, half:] = hot_sum[:, :half]
    send[:, :half] = (block_sum[:, half:] + neg_send).astype(BF16)
    send[:, half:] = hot_sum[:, half:].astype(BF16)
    kind[:width, :] = kind_sum.astype(BF16)
    kind[width:, :] = jnp.zeros((kind.shape[0] - width, kind.shape[1]), BF16)


def add_kernel(keep, got, out):
    width = keep.shape[0]
    out[:width, :] = (keep[...] + got[...].astype(F32)).astype(BF16)
    out[width:, :] = jnp.zeros((out.shape[0] - width, out.shape[1]), BF16)


def chunk_sum(ref, lanes, peers):
    rows = ref.shape[0] // PEERS
    total = 0.0
    for peer in peers:
        total = total + ref[peer * rows : (peer + 1) * rows, lanes].astype(F32)
    return total


def bucket_kernel(got, kind, out, own):
    rows = got.shape[0] // PEERS
    half = kind.shape[1]
    everyone = range(PEERS)
    own[...] = chunk_sum(got, slice(0, half), everyone)
    hot = chunk_sum(got, slice(half, 2 * half), everyone).astype(BF16)
    out[:, :half] = kind[...]
    for peer in everyone:
        out[peer * rows : (peer + 1) * rows, half:] = hot


def spread_kernel(got, own, out, kind):
    rows = got.shape[0] // PEERS
    half = own.shape[1]
    own_sum = own[...].astype(BF16)
    parts = []
    for side in range(2):
        peers = range(side * PEERS // 2, (side + 1) * PEERS // 2)
        parts.append(chunk_sum(got, slice(0, 2 * half), peers).astype(BF16))
    for peer in range(PEERS):
        at = slice(peer * rows, (peer + 1) * rows)
        out[at, :half] = own_sum
        for side, part in enumerate(parts):
            out[at, (side + 1) * half : (side + 2) * half] = part[:, half:]
            kind[at, side * half : (side + 1) * half] = part[:, :half]


def adagrad(weights, state, grads, new_weights, new_state, at):
    total = state[:, at] + jnp.sum(grads * grads, axis=0, keepdims=True) / grads.shape[0]
    new_state[:, at] = total
    new_weights[:, at] = weights[:, at] - grads * (STEP / (jnp.sqrt(total) + EPS))


def entity_kernel(mine, other, block, block_state, hot, hot_state, new_b, new_bs, new_h, new_hs):
    width, rows = block.shape
    half = rows // 2
    first = core_of() == 0
    for core in range(2):
        from_mine = first if core == 0 else jnp.logical_not(first)
        grads = jnp.where(from_mine, mine[:width, :], other[:width, :]).astype(F32)
        at = slice(core * half, (core + 1) * half)
        adagrad(block, block_state, grads[:, :half], new_b, new_bs, at)
        for side in range(2):
            at = slice(side * rows + core * half, side * rows + (core + 1) * half)
            part = grads[:, (side + 1) * half : (side + 2) * half]
            adagrad(hot, hot_state, part, new_h, new_hs, at)


def relation_kernel(grads, weights, state, new_weights, new_state):
    width, rows = weights.shape
    adagrad(weights, state, grads[:width, :].astype(F32), new_weights, new_state, slice(0, rows))


def flipped(x, axis, bit):
    return lax.ppermute(x, axis, [(i, i ^ bit) for i in range(lax.axis_size(axis))])


def exchanged(x, axis, groups=None):
    return lax.all_to_all(x, axis, 0, 0, tiled=True, axis_index_groups=groups)


def local(
    entity_block,
    block_state,
    hot_entities,
    hot_state,
    relations,
    relation_state,
    source_ids,
    target_ids,
    relation_ids,
    negative_ids,
):
    rows, width = entity_block.shape
    hot_rows = hot_entities.shape[0]
    edges = source_ids.shape[1]
    padded = -(-width // 256) * 256
    slot = padded // PEERS
    half = rows // 2
    block_t, hot_t, rel_t = entity_block.T, hot_entities.T, relations.T
    own_bf, ids = call(
        pack_kernel,
        [((width, rows), BF16), ((8, 1024), jnp.int32)],
        (block_t, source_ids, target_ids, relation_ids, negative_ids.reshape(1, -1)),
    )
    swap = lax.axis_size("bucket") // 2
    partner = flipped(own_bf, "bucket", swap)
    far_ids = flipped(ids, "bucket", swap)
    src, rel_rows, dst_hot, hot_bf, rel_bf = call(
        gather_kernel,
        [((width, edges), BF16)] * 3 + [((width, hot_rows), BF16), ((width, rows), BF16)],
        (own_bf, hot_t, rel_t, ids),
        1 << 30,
    )
    keep, send, kind = call(
        grad_kernel,
        [((width, rows), F32), ((width, rows), BF16), ((padded, half), BF16)],
        (own_bf, partner, hot_bf, rel_bf, src, rel_rows, dst_hot, ids, far_ids),
        1 << 31,
    )
    pairs = [[2 * i + core for i in range(PEERS)] for core in range(2)]
    (mixed,) = call(add_kernel, [((padded, rows), BF16)], (keep, flipped(send, "edge", 1)))
    mixed = exchanged(mixed, "edge", pairs)
    to_bucket, own_part = call(
        bucket_kernel, [((padded, rows), BF16), ((slot, half), F32)], (mixed, kind)
    )
    from_bucket = exchanged(to_bucket, "bucket")
    entity_part, kind_part = call(
        spread_kernel, [((padded, 3 * half), BF16), ((padded, rows), BF16)], (from_bucket, own_part)
    )
    mine = exchanged(entity_part, "edge", pairs)
    mine, kind_part = lax.optimization_barrier((mine, kind_part))
    other = flipped(mine, "edge", 1)
    kind_grads = exchanged(kind_part, "bucket")
    new_block, new_block_state, new_hot, new_hot_state = call(
        entity_kernel,
        [((width, rows), F32), ((1, rows), F32), ((width, hot_rows), F32), ((1, hot_rows), F32)],
        (mine, other, block_t, block_state.reshape(1, -1), hot_t, hot_state.reshape(1, -1)),
    )
    new_relations, new_relation_state = call(
        relation_kernel,
        [((width, rows), F32), ((1, rows), F32)],
        (kind_grads, rel_t, relation_state.reshape(1, -1)),
    )
    return (
        new_block.T,
        new_block_state.reshape(-1),
        new_hot.T,
        new_hot_state.reshape(-1),
        new_relations.T,
        new_relation_state.reshape(-1),
    )


def solution(mesh):
    placed = (
        P("bucket", None),
        P("bucket"),
        P(),
        P(),
        P("edge", None),
        P("edge"),
        P("bucket", "edge"),
        P("bucket", "edge"),
        P("bucket", "edge"),
        P("bucket", "edge", None),
    )
    return jax.shard_map(
        local,
        mesh=mesh,
        in_specs=placed,
        out_specs=(P("bucket", None), P("bucket"), P(), P(), P("edge", None), P("edge")),
        check_vma=False,
    )
```

```python
import functools

import jax
import jax.numpy as jnp
from jax import lax
from jax.experimental import pallas as pl
from jax.experimental.pallas import tpu as pltpu
from jax.sharding import PartitionSpec as P

STEP = 0.3
EPS = 1e-06
F32 = jnp.float32
BF16 = jnp.bfloat16
PEERS = 16
WORD = 256
VMEM = pl.BlockSpec(memory_space=pltpu.VMEM)


def call(body, outs, args, flops=1 << 22, specs=None, scratch=()):
    moved = sum(a.size * a.dtype.itemsize for a in args)
    return pl.pallas_call(
        body,
        out_shape=[jax.ShapeDtypeStruct(shape, dtype) for shape, dtype in outs],
        in_specs=specs or [VMEM] * len(args),
        out_specs=[VMEM] * len(outs),
        scratch_shapes=scratch,
        compiler_params=pltpu.CompilerParams(vmem_limit_bytes=32 << 20),
        cost_estimate=pl.CostEstimate(flops=flops, bytes_accessed=moved, transcendentals=0),
    )(*args)


def one_hot(ids, rows):
    grid = lax.broadcasted_iota(jnp.int32, (rows, ids.shape[1]), 0)
    return jnp.where(grid == ids, 1.0, 0.0).astype(BF16)


def mm(a, b):
    return lax.dot_general(a, b, (((1,), (0,)), ((), ())), preferred_element_type=F32)


def mm_t(a, b):
    return lax.dot_general(a, b, (((1,), (1,)), ((), ())), preferred_element_type=F32)


def core_of():
    return lax.axis_index("edge") & 1


def pieces(length):
    return [(at, min(WORD, length - at)) for at in range(0, length, WORD)]


def id_plan(edges, negatives):
    plan, row = [], 0
    for which, length, digits in ((0, edges, 2), (1, edges, 2), (2, edges, 1), (3, negatives, 1)):
        for digit in range(digits):
            plan.append((which, digit, row, length))
            row += len(pieces(length))
    return plan, -(-row // 32) * 32


def pack_kernel(block, src_ids, dst_ids, rel_ids, neg_ids, table, in_block, *scratch):
    held, sems, rows_f = scratch[:4], scratch[4], scratch[5]
    sources = (src_ids, dst_ids, rel_ids, neg_ids)
    copies = [pltpu.make_async_copy(block, in_block, sems.at[4])]
    for at, (source, target) in enumerate(zip(sources, held)):
        copies.append(pltpu.make_async_copy(source, target, sems.at[at]))
    for copy in copies:
        copy.start()
    for copy in copies[1:]:
        copy.wait()
    width = block.shape[0]
    plan, _ = id_plan(src_ids.shape[1], neg_ids.shape[1])
    rows_f[...] = jnp.full(rows_f.shape, -1.0, F32)
    for which, digit, row, length in plan:
        ids = held[which][...]
        ids = ids >> 8 if digit else ids & 255
        for step, (at, size) in enumerate(pieces(length)):
            rows_f[row + step : row + step + 1, :size] = ids[:, at : at + size].astype(F32)
    table[width:, :] = rows_f[...].astype(BF16)
    copies[0].wait()
    table[:width, :] = in_block[...].astype(BF16)


def unpack(table, width, edges, negatives):
    plan, _ = id_plan(edges, negatives)
    rows_f = table[width:, :].astype(F32)
    out = [None] * 4
    for which, digit, row, length in plan:
        parts = [
            rows_f[row + step : row + step + 1, : -(-size // 128) * 128]
            for step, (_, size) in enumerate(pieces(length))
        ]
        ids = jnp.concatenate(parts, axis=1).astype(jnp.int32)
        out[which] = out[which] + ids * 256 if digit else ids
    return out


def gather_kernel(negatives, own, hot, rel, src_out, rel_out, dst_out, hot_bf, rel_bf):
    width, rows = hot.shape[0], own.shape[1]
    hot_rows = hot.shape[1]
    src_at, dst_at, rel_at, _ = unpack(own, width, src_out.shape[1], negatives)
    hot_bf[...] = hot[...].astype(BF16)
    rel_bf[...] = rel[...].astype(BF16)
    src_out[...] = (
        mm(own[:width, :], one_hot(src_at, rows))
        + mm(hot_bf[...], one_hot(src_at - rows, hot_rows))
    ).astype(BF16)
    rel_out[...] = mm(rel_bf[...], one_hot(rel_at, rel.shape[1])).astype(BF16)
    dst_out[...] = mm(hot_bf[...], one_hot(dst_at - rows, hot_rows)).astype(BF16)


def edge_grads(partner, src, rel, dst, neg_at):
    query = (src * rel).astype(BF16)
    query_f = query.astype(F32)
    positive = jnp.sum(query_f * dst, axis=0, keepdims=True)
    pos_grad = -1.0 / (1.0 + jnp.exp(positive))
    scores = mm(partner.T, query)
    sig = (1.0 / (1.0 + jnp.exp(-scores))).astype(BF16)
    named = one_hot(neg_at, partner.shape[1])
    count = mm_t(jnp.ones((8, neg_at.shape[1]), BF16), named)[:1, :]
    scaled = partner.astype(F32) * count
    high = scaled.astype(BF16)
    low = (scaled - high.astype(F32)).astype(BF16)
    query_grad = pos_grad * dst + mm(high, sig) + mm(low, sig)
    src_grad = (query_grad * rel).astype(BF16)
    kind_grad = (query_grad * src).astype(BF16)
    dst_grad = (pos_grad * query_f).astype(BF16)
    return query, sig, count, src_grad, kind_grad, dst_grad


def grad_kernel(negatives, own, partner, hot, rel, src, rel_rows, dst_hot, keep, send):
    width, edges = src.shape
    rows, hot_rows = own.shape[1], hot.shape[1]
    half = rows // 2
    side = lax.axis_index("bucket") // (lax.axis_size("bucket") // 2)
    own_table, partner_table = own[:width, :], partner[:width, :]

    def hot_hits(at):
        at = at - rows - side * rows
        return one_hot(at, rows)

    src_at, dst_at, rel_at, neg_at = unpack(own, width, edges, negatives)
    dst = mm(partner_table, one_hot(dst_at, rows)) + dst_hot[...].astype(F32)
    _, _, _, src_grad, kind_grad, dst_grad = edge_grads(
        partner_table, src[...].astype(F32), rel_rows[...].astype(F32), dst, neg_at
    )
    block_sum = mm_t(src_grad, one_hot(src_at, rows))
    hot_sum = mm_t(src_grad, hot_hits(src_at))
    hot_sum += mm_t(dst_grad, hot_hits(dst_at))
    kind_sum = mm_t(kind_grad, one_hot(rel_at - side * half, half))

    src_at, dst_at, rel_at, neg_at = unpack(partner, width, edges, negatives)
    far_src = mm(partner_table, one_hot(src_at, rows)) + mm(
        hot[...], one_hot(src_at - rows, hot_rows)
    )
    far_dst = mm(own_table, one_hot(dst_at, rows)) + mm(hot[...], one_hot(dst_at - rows, hot_rows))
    far_rel = mm(rel[...], one_hot(rel_at, rel.shape[1]))
    query, sig, count, src_grad, kind_grad, dst_grad = edge_grads(
        own_table, far_src, far_rel, far_dst, neg_at
    )
    block_sum += mm_t(query, sig) * count
    block_sum += mm_t(dst_grad, one_hot(dst_at, rows))
    hot_sum += mm_t(src_grad, hot_hits(src_at))
    hot_sum += mm_t(dst_grad, hot_hits(dst_at))
    kind_sum += mm_t(kind_grad, one_hot(rel_at - side * half, half))

    @pl.when(core_of() == 0)
    def _():
        keep[:, :rows] = block_sum
        keep[:, rows:] = hot_sum
        send[:, :half] = kind_sum.astype(BF16)
        send[:, half:] = jnp.zeros((width, send.shape[1] - half), BF16)

    @pl.when(core_of() == 1)
    def _():
        keep[:, :half] = kind_sum
        keep[:, half:] = jnp.zeros((width, keep.shape[1] - half), F32)
        send[:, :rows] = block_sum.astype(BF16)
        send[:, rows:] = hot_sum.astype(BF16)


def merge_kernel(keep, got, out):
    width, lanes = keep.shape
    half = lanes // 4
    out[width:, :] = jnp.zeros((out.shape[0] - width, lanes), BF16)

    @pl.when(core_of() == 0)
    def _():
        out[:width, :] = (keep[...] + got[...].astype(F32)).astype(BF16)

    @pl.when(core_of() == 1)
    def _():
        out[:width, :half] = got[:, :half]
        out[:width, half : 2 * half] = keep[:, :half].astype(BF16)
        out[:width, 2 * half :] = jnp.zeros((width, 2 * half), BF16)


def chunk_sum(ref, lanes, peers):
    rows = ref.shape[0] // PEERS
    total = 0.0
    for peer in peers:
        total = total + ref[peer * rows : (peer + 1) * rows, lanes].astype(F32)
    return total


SIDES = (range(PEERS // 2), range(PEERS // 2, PEERS))


def first_kernel(got, out, held):
    rows = got.shape[0] // PEERS
    lanes = out.shape[1]
    half = lanes // 2

    @pl.when(core_of() == 0)
    def _():
        held[:, :lanes] = chunk_sum(got, slice(0, lanes), range(PEERS)).astype(BF16)
        held[:, lanes:] = jnp.zeros((rows, lanes), BF16)
        hot = chunk_sum(got, slice(lanes, 2 * lanes), range(PEERS)).astype(BF16)
        for peer in range(PEERS):
            out[peer * rows : (peer + 1) * rows, :] = hot

    @pl.when(core_of() == 1)
    def _():
        for side, peers in enumerate(SIDES):
            part = chunk_sum(got, slice(0, lanes), peers).astype(BF16)
            for core in range(2):
                at = core * lanes + side * half
                held[:, at : at + half] = part[:, core * half : (core + 1) * half]
        out[...] = jnp.zeros(out.shape, BF16)


def second_kernel(got, held, out):
    rows = got.shape[0] // PEERS
    lanes = got.shape[1]

    @pl.when(core_of() == 0)
    def _():
        parts = [held[:, :lanes]]
        parts += [chunk_sum(got, slice(0, lanes), peers).astype(BF16) for peers in SIDES]
        for peer in range(PEERS):
            for at, part in enumerate(parts):
                out[peer * rows : (peer + 1) * rows, at * lanes : (at + 1) * lanes] = part

    @pl.when(core_of() == 1)
    def _():
        for peer in range(PEERS):
            out[peer * rows : (peer + 1) * rows, : 2 * lanes] = held[...]
            out[peer * rows : (peer + 1) * rows, 2 * lanes :] = jnp.zeros((rows, lanes), BF16)


def adagrad(weights, state, grads, new_weights, new_state, at):
    total = state[:, at] + jnp.sum(grads * grads, axis=0, keepdims=True) / grads.shape[0]
    new_state[:, at] = total
    new_weights[:, at] = weights[:, at] - grads * (STEP / (jnp.sqrt(total) + EPS))


def update_kernel(
    mine, other, block, block_s, hot, hot_s, rel, rel_s, new_b, new_bs, new_h, new_hs, new_r, new_rs
):
    width, rows = block.shape
    first = core_of() == 0
    for part in range(3):
        at = slice(part * rows, (part + 1) * rows)
        grads = jnp.where(first, mine[:width, at], other[:width, at]).astype(F32)
        if part == 0:
            adagrad(block, block_s, grads, new_b, new_bs, slice(0, rows))
        else:
            adagrad(hot, hot_s, grads, new_h, new_hs, slice((part - 1) * rows, part * rows))
    grads = jnp.where(first, other[:width, :rows], mine[:width, rows : 2 * rows]).astype(F32)
    adagrad(rel, rel_s, grads, new_r, new_rs, slice(0, rows))


def flipped(x, axis, bit):
    return lax.ppermute(x, axis, [(i, i ^ bit) for i in range(lax.axis_size(axis))])


def exchanged(x, groups):
    return lax.all_to_all(x, ("bucket", "edge"), 0, 0, tiled=True, axis_index_groups=groups)


def edge_groups(core):
    n = lax.axis_size("edge")
    return [[b * n + e for e in range(core, n, 2)] for b in range(lax.axis_size("bucket"))]


def bucket_groups(core):
    n = lax.axis_size("edge")
    return [[b * n + e for b in range(lax.axis_size("bucket"))] for e in range(core, n, 2)]


def local(
    entity_block,
    block_state,
    hot_entities,
    hot_state,
    relations,
    relation_state,
    source_ids,
    target_ids,
    relation_ids,
    negative_ids,
):
    rows, width = entity_block.shape
    hot_rows = hot_entities.shape[0]
    edges = source_ids.shape[1]
    padded = -(-width // 256) * 256
    slot = padded // PEERS
    block_t, hot_t, rel_t = entity_block.T, hot_entities.T, relations.T
    negatives = negative_ids.shape[-1]
    ids = (source_ids, target_ids, relation_ids, negative_ids.reshape(1, -1))
    _, id_height = id_plan(edges, negatives)
    (own,) = call(
        pack_kernel,
        [((width + id_height, rows), BF16)],
        (block_t, *ids),
        specs=[pl.BlockSpec(memory_space=pl.ANY)] * 5,
        scratch=[pltpu.VMEM((width, rows), F32)]
        + [pltpu.VMEM(part.shape, jnp.int32) for part in ids]
        + [pltpu.SemaphoreType.DMA((5,)), pltpu.VMEM((id_height, rows), F32)],
    )
    partner = flipped(own, "bucket", lax.axis_size("bucket") // 2)
    src, rel_rows, dst_hot, hot_bf, rel_bf = call(
        functools.partial(gather_kernel, negatives),
        [((width, edges), BF16)] * 3 + [((width, hot_rows), BF16), ((width, rows), BF16)],
        (own, hot_t, rel_t),
        1 << 30,
    )
    keep, send = call(
        functools.partial(grad_kernel, negatives),
        [((width, 2 * rows), F32), ((width, 2 * rows), BF16)],
        (own, partner, hot_bf, rel_bf, src, rel_rows, dst_hot),
        1 << 31,
    )
    both = edge_groups(0) + bucket_groups(1)
    (mixed,) = call(
        merge_kernel, [((padded, 2 * rows), BF16)], (keep, flipped(send, "edge", 1))
    )
    mixed = exchanged(mixed, both)
    hot_part, held = call(
        first_kernel, [((padded, rows), BF16), ((slot, 2 * rows), BF16)], (mixed,)
    )
    hot_part = exchanged(hot_part, bucket_groups(0) + edge_groups(1))
    (totals,) = call(second_kernel, [((padded, 3 * rows), BF16)], (hot_part, held))
    mine = exchanged(totals, both)
    other = flipped(mine, "edge", 1)
    shapes = [(width, rows), (1, rows), (width, hot_rows), (1, hot_rows), (width, rows), (1, rows)]
    new_block, new_block_state, new_hot, new_hot_state, new_relations, new_relation_state = call(
        update_kernel,
        [(shape, F32) for shape in shapes],
        (
            mine,
            other,
            block_t,
            block_state.reshape(1, -1),
            hot_t,
            hot_state.reshape(1, -1),
            rel_t,
            relation_state.reshape(1, -1),
        ),
    )
    return (
        new_block.T,
        new_block_state.reshape(-1),
        new_hot.T,
        new_hot_state.reshape(-1),
        new_relations.T,
        new_relation_state.reshape(-1),
    )


def solution(mesh):
    placed = (
        P("bucket", None),
        P("bucket"),
        P(),
        P(),
        P("edge", None),
        P("edge"),
        P("bucket", "edge"),
        P("bucket", "edge"),
        P("bucket", "edge"),
        P("bucket", "edge", None),
    )
    return jax.shard_map(
        local,
        mesh=mesh,
        in_specs=placed,
        out_specs=(P("bucket", None), P("bucket"), P(), P(), P("edge", None), P("edge")),
        check_vma=False,
    )
```

```python
import functools

import jax
import jax.numpy as jnp
from jax import lax
from jax.experimental import pallas as pl
from jax.experimental.pallas import tpu as pltpu
from jax.sharding import PartitionSpec as P

STEP = 0.3
EPS = 1e-06
F32 = jnp.float32
BF16 = jnp.bfloat16
PEERS = 16
WORD = 256
VMEM = pl.BlockSpec(memory_space=pltpu.VMEM)
HBM = pl.BlockSpec(memory_space=pltpu.HBM)


def call(body, outs, args, flops=1 << 22, specs=None, out_specs=None, scratch=(), room=32):
    moved = sum(a.size * a.dtype.itemsize for a in args)
    return pl.pallas_call(
        body,
        out_shape=[jax.ShapeDtypeStruct(shape, dtype) for shape, dtype in outs],
        in_specs=specs or [VMEM] * len(args),
        out_specs=out_specs or [VMEM] * len(outs),
        scratch_shapes=scratch,
        compiler_params=pltpu.CompilerParams(vmem_limit_bytes=room << 20),
        cost_estimate=pl.CostEstimate(flops=flops, bytes_accessed=moved, transcendentals=0),
    )(*args)


def one_hot(ids, rows):
    grid = lax.broadcasted_iota(jnp.int32, (rows, ids.shape[1]), 0)
    return jnp.where(grid == ids, 1.0, 0.0).astype(BF16)


def mm(a, b):
    return lax.dot_general(a, b, (((1,), (0,)), ((), ())), preferred_element_type=F32)


def mm_t(a, b):
    return lax.dot_general(a, b, (((1,), (1,)), ((), ())), preferred_element_type=F32)


def core_of():
    return lax.axis_index("edge") & 1


def pieces(length):
    return [(at, min(WORD, length - at)) for at in range(0, length, WORD)]


def id_plan(edges, negatives):
    plan, row = [], 0
    for which, length, digits in ((0, edges, 2), (1, edges, 2), (2, edges, 1), (3, negatives, 1)):
        for digit in range(digits):
            plan.append((which, digit, row, length))
            row += len(pieces(length))
    return plan, -(-row // 32) * 32


def pack_kernel(block, src_ids, dst_ids, rel_ids, neg_ids, table, in_block, *scratch):
    held, sems, rows_f = scratch[:4], scratch[4], scratch[5]
    sources = (src_ids, dst_ids, rel_ids, neg_ids)
    copies = [pltpu.make_async_copy(block, in_block, sems.at[4])]
    for at, (source, target) in enumerate(zip(sources, held)):
        copies.append(pltpu.make_async_copy(source, target, sems.at[at]))
    for copy in copies:
        copy.start()
    for copy in copies[1:]:
        copy.wait()
    width = block.shape[0]
    plan, _ = id_plan(src_ids.shape[1], neg_ids.shape[1])
    rows_f[...] = jnp.full(rows_f.shape, -1.0, F32)
    for which, digit, row, length in plan:
        ids = held[which][...]
        ids = ids >> 8 if digit else ids & 255
        for step, (at, size) in enumerate(pieces(length)):
            rows_f[row + step : row + step + 1, :size] = ids[:, at : at + size].astype(F32)
    table[width:, :] = rows_f[...].astype(BF16)
    copies[0].wait()
    table[:width, :] = in_block[...].astype(BF16)


def unpack(table, width, edges, negatives):
    plan, _ = id_plan(edges, negatives)
    rows_f = table[width:, :].astype(F32)
    out = [None] * 4
    for which, digit, row, length in plan:
        parts = [
            rows_f[row + step : row + step + 1, : -(-size // 128) * 128]
            for step, (_, size) in enumerate(pieces(length))
        ]
        ids = jnp.concatenate(parts, axis=1).astype(jnp.int32)
        out[which] = out[which] + ids * 256 if digit else ids
    return out


def gather_kernel(
    negatives, own, hot, rel, block_s, hot_s, rel_s, src_out, rel_out, dst_out, hot_bf, rel_bf, states
):
    width, rows = hot.shape[0], own.shape[1]
    states[...] = jnp.zeros(states.shape, F32)
    for at, state in enumerate((block_s, hot_s, rel_s)):
        states[at : at + 1, : state.shape[1]] = state[...]
    hot_rows = hot.shape[1]
    src_at, dst_at, rel_at, _ = unpack(own, width, src_out.shape[1], negatives)
    hot_bf[...] = hot[...].astype(BF16)
    rel_bf[...] = rel[...].astype(BF16)
    src_out[...] = (
        mm(own[:width, :], one_hot(src_at, rows))
        + mm(hot_bf[...], one_hot(src_at - rows, hot_rows))
    ).astype(BF16)
    rel_out[...] = mm(rel_bf[...], one_hot(rel_at, rel.shape[1])).astype(BF16)
    dst_out[...] = mm(hot_bf[...], one_hot(dst_at - rows, hot_rows)).astype(BF16)


def edge_grads(partner, src, rel, dst, neg_at):
    query = (src * rel).astype(BF16)
    query_f = query.astype(F32)
    positive = jnp.sum(query_f * dst, axis=0, keepdims=True)
    pos_grad = -1.0 / (1.0 + jnp.exp(positive))
    scores = mm(partner.T, query)
    sig = (1.0 / (1.0 + jnp.exp(-scores))).astype(BF16)
    named = one_hot(neg_at, partner.shape[1])
    count = mm_t(jnp.ones((8, neg_at.shape[1]), BF16), named)[:1, :]
    scaled = partner.astype(F32) * count
    high = scaled.astype(BF16)
    low = (scaled - high.astype(F32)).astype(BF16)
    query_grad = pos_grad * dst + mm(high, sig) + mm(low, sig)
    src_grad = (query_grad * rel).astype(BF16)
    kind_grad = (query_grad * src).astype(BF16)
    dst_grad = (pos_grad * query_f).astype(BF16)
    return query, sig, count, src_grad, kind_grad, dst_grad


def grad_kernel(negatives, own, partner, hot, rel, src, rel_rows, dst_hot, keep, send):
    width, edges = src.shape
    rows, hot_rows = own.shape[1], hot.shape[1]
    half = rows // 2
    side = lax.axis_index("bucket") // (lax.axis_size("bucket") // 2)
    own_table, partner_table = own[:width, :], partner[:width, :]

    def hot_hits(at):
        return one_hot(at - rows - side * rows, rows)

    near_src, near_dst, near_rel, near_neg = unpack(own, width, edges, negatives)
    dst = mm(partner_table, one_hot(near_dst, rows)) + dst_hot[...].astype(F32)
    _, _, _, near_src_grad, near_kind_grad, near_dst_grad = edge_grads(
        partner_table, src[...].astype(F32), rel_rows[...].astype(F32), dst, near_neg
    )
    far_src, far_dst, far_rel, far_neg = unpack(partner, width, edges, negatives)
    ends = jnp.concatenate([far_src, far_dst], axis=1)
    from_hot = mm(hot[...], one_hot(ends - rows, hot_rows))
    src_rows = mm(partner_table, one_hot(far_src, rows)) + from_hot[:, :edges]
    dst_rows = mm(own_table, one_hot(far_dst, rows)) + from_hot[:, edges:]
    kind_rows = mm(rel[...], one_hot(far_rel, rel.shape[1]))
    query, sig, count, far_src_grad, far_kind_grad, far_dst_grad = edge_grads(
        own_table, src_rows, kind_rows, dst_rows, far_neg
    )
    cold = jnp.concatenate([near_src_grad, far_dst_grad], axis=1)
    cold_at = jnp.concatenate([near_src, far_dst], axis=1)
    block_sum = mm_t(query, sig) * count + mm_t(cold, one_hot(cold_at, rows))
    named = jnp.concatenate([near_dst_grad, cold, far_src_grad], axis=1)
    named_at = jnp.concatenate([near_dst, cold_at, far_src], axis=1)
    hot_sum = mm_t(named, hot_hits(named_at))
    kind_grad = jnp.concatenate([near_kind_grad, far_kind_grad], axis=1)
    kind_at = jnp.concatenate([near_rel, far_rel], axis=1)
    kind_sum = mm_t(kind_grad, one_hot(kind_at - side * half, half))

    @pl.when(core_of() == 0)
    def _():
        keep[:, :rows] = block_sum
        keep[:, rows:] = hot_sum
        send[:, :half] = kind_sum.astype(BF16)
        send[:, half:] = jnp.zeros((width, send.shape[1] - half), BF16)

    @pl.when(core_of() == 1)
    def _():
        keep[:, :half] = kind_sum
        keep[:, half:] = jnp.zeros((width, keep.shape[1] - half), F32)
        send[:, :rows] = block_sum.astype(BF16)
        send[:, rows:] = hot_sum.astype(BF16)


def merge_kernel(keep, got, out):
    width, lanes = keep.shape
    half = lanes // 4
    out[width:, :] = jnp.zeros((out.shape[0] - width, lanes), BF16)

    @pl.when(core_of() == 0)
    def _():
        out[:width, :] = (keep[...] + got[...].astype(F32)).astype(BF16)

    @pl.when(core_of() == 1)
    def _():
        out[:width, :half] = got[:, :half]
        out[:width, half : 2 * half] = keep[:, :half].astype(BF16)
        out[:width, 2 * half :] = jnp.zeros((width, 2 * half), BF16)


def chunk_sum(ref, lanes, peers):
    rows = ref.shape[0] // PEERS
    total = 0.0
    for peer in peers:
        total = total + ref[peer * rows : (peer + 1) * rows, lanes].astype(F32)
    return total


SIDES = (range(PEERS // 2), range(PEERS // 2, PEERS))


def first_kernel(got, out, held):
    rows = got.shape[0] // PEERS
    lanes = out.shape[1]
    half = lanes // 2

    @pl.when(core_of() == 0)
    def _():
        held[:, :lanes] = chunk_sum(got, slice(0, lanes), range(PEERS)).astype(BF16)
        held[:, lanes:] = jnp.zeros((rows, lanes), BF16)
        hot = chunk_sum(got, slice(lanes, 2 * lanes), range(PEERS)).astype(BF16)
        for peer in range(PEERS):
            out[peer * rows : (peer + 1) * rows, :] = hot

    @pl.when(core_of() == 1)
    def _():
        for side, peers in enumerate(SIDES):
            part = chunk_sum(got, slice(0, lanes), peers).astype(BF16)
            for core in range(2):
                at = core * lanes + side * half
                held[:, at : at + half] = part[:, core * half : (core + 1) * half]
        out[...] = jnp.zeros(out.shape, BF16)


def second_kernel(got, held, out):
    rows = got.shape[0] // PEERS
    lanes = got.shape[1]

    @pl.when(core_of() == 0)
    def _():
        parts = [held[:, :lanes]]
        parts += [chunk_sum(got, slice(0, lanes), peers).astype(BF16) for peers in SIDES]
        for peer in range(PEERS):
            for at, part in enumerate(parts):
                out[peer * rows : (peer + 1) * rows, at * lanes : (at + 1) * lanes] = part

    @pl.when(core_of() == 1)
    def _():
        for peer in range(PEERS):
            out[peer * rows : (peer + 1) * rows, : 2 * lanes] = held[...]
            out[peer * rows : (peer + 1) * rows, 2 * lanes :] = jnp.zeros((rows, lanes), BF16)


def update_kernel(mine, other, states, block, hot, rel, *refs):
    outs, state_outs, helds, state_held, sems = refs[:3], refs[3:6], refs[6:9], refs[9], refs[10]
    width, rows = block.shape
    first = core_of() == 0
    copies = []
    state_held[...] = states[...]
    for table, weights in enumerate((block, hot, rel)):
        for low in range(0, weights.shape[1], rows):
            at = slice(low, low + rows)
            if table < 2:
                lanes = slice(table * rows + low, (table + 1) * rows + low)
                grads = jnp.where(first, mine[:width, lanes], other[:width, lanes])
            else:
                grads = jnp.where(first, other[:width, :rows], mine[:width, rows : 2 * rows])
            grads = grads.astype(F32)
            total = states[table : table + 1, at] + jnp.sum(grads * grads, axis=0, keepdims=True) / width
            state_held[table : table + 1, at] = total
            helds[table][:, at] = weights[:, at] - grads * (STEP / (jnp.sqrt(total) + EPS))
        state = state_held.at[table : table + 1, : weights.shape[1]]
        copies.append(pltpu.make_async_copy(helds[table], outs[table], sems.at[2 * table]))
        copies.append(pltpu.make_async_copy(state, state_outs[table], sems.at[2 * table + 1]))
        copies[-2].start()
        copies[-1].start()
    for copy in copies:
        copy.wait()


def flipped(x, axis, bit):
    return lax.ppermute(x, axis, [(i, i ^ bit) for i in range(lax.axis_size(axis))])


def exchanged(x, groups):
    return lax.all_to_all(x, ("bucket", "edge"), 0, 0, tiled=True, axis_index_groups=groups)


def edge_groups(core):
    n = lax.axis_size("edge")
    return [[b * n + e for e in range(core, n, 2)] for b in range(lax.axis_size("bucket"))]


def bucket_groups(core):
    n = lax.axis_size("edge")
    return [[b * n + e for b in range(lax.axis_size("bucket"))] for e in range(core, n, 2)]


def local(
    entity_block,
    block_state,
    hot_entities,
    hot_state,
    relations,
    relation_state,
    source_ids,
    target_ids,
    relation_ids,
    negative_ids,
):
    rows, width = entity_block.shape
    hot_rows = hot_entities.shape[0]
    edges = source_ids.shape[1]
    padded = -(-width // 256) * 256
    slot = padded // PEERS
    block_t, hot_t, rel_t = entity_block.T, hot_entities.T, relations.T
    negatives = negative_ids.shape[-1]
    ids = (source_ids, target_ids, relation_ids, negative_ids.reshape(1, -1))
    _, id_height = id_plan(edges, negatives)
    (own,) = call(
        pack_kernel,
        [((width + id_height, rows), BF16)],
        (block_t, *ids),
        specs=[HBM] * 5,
        room=63,
        scratch=[pltpu.VMEM((width, rows), F32)]
        + [pltpu.VMEM(part.shape, jnp.int32) for part in ids]
        + [pltpu.SemaphoreType.DMA((5,)), pltpu.VMEM((id_height, rows), F32)],
    )
    partner = flipped(own, "bucket", lax.axis_size("bucket") // 2)
    state_rows = [state.reshape(1, -1) for state in (block_state, hot_state, relation_state)]
    src, rel_rows, dst_hot, hot_bf, rel_bf, states = call(
        functools.partial(gather_kernel, negatives),
        [((width, edges), BF16)] * 3
        + [((width, hot_rows), BF16), ((width, rows), BF16), ((8, hot_rows), F32)],
        (own, hot_t, rel_t, *state_rows),
        1 << 30,
    )
    keep, send = call(
        functools.partial(grad_kernel, negatives),
        [((width, 2 * rows), F32), ((width, 2 * rows), BF16)],
        (own, partner, hot_bf, rel_bf, src, rel_rows, dst_hot),
        1 << 31,
    )
    both = edge_groups(0) + bucket_groups(1)
    (mixed,) = call(
        merge_kernel, [((padded, 2 * rows), BF16)], (keep, flipped(send, "edge", 1))
    )
    mixed = exchanged(mixed, both)
    hot_part, held = call(
        first_kernel, [((padded, rows), BF16), ((slot, 2 * rows), BF16)], (mixed,)
    )
    hot_part = exchanged(hot_part, bucket_groups(0) + edge_groups(1))
    (totals,) = call(second_kernel, [((padded, 3 * rows), BF16)], (hot_part, held))
    mine = exchanged(totals, both)
    other = flipped(mine, "edge", 1)
    tables = (block_t, hot_t, rel_t)
    new_block, new_hot, new_relations, *new_states = call(
        update_kernel,
        [(part.shape, F32) for part in (*tables, *state_rows)],
        (mine, other, states, *tables),
        out_specs=[HBM] * 6,
        scratch=[pltpu.VMEM(part.shape, F32) for part in (*tables, states)]
        + [pltpu.SemaphoreType.DMA((6,))],
    )
    new_block_state, new_hot_state, new_relation_state = [part.reshape(-1) for part in new_states]
    return (
        new_block.T,
        new_block_state,
        new_hot.T,
        new_hot_state,
        new_relations.T,
        new_relation_state,
    )


def solution(mesh):
    placed = (
        P("bucket", None),
        P("bucket"),
        P(),
        P(),
        P("edge", None),
        P("edge"),
        P("bucket", "edge"),
        P("bucket", "edge"),
        P("bucket", "edge"),
        P("bucket", "edge", None),
    )
    return jax.shard_map(
        local,
        mesh=mesh,
        in_specs=placed,
        out_specs=(P("bucket", None), P("bucket"), P(), P(), P("edge", None), P("edge")),
        check_vma=False,
    )
```

```python
import functools

import jax
import jax.numpy as jnp
from jax import lax
from jax.experimental import pallas as pl
from jax.experimental.pallas import tpu as pltpu
from jax.sharding import PartitionSpec as P

STEP = 0.3
EPS = 1e-06
F32 = jnp.float32
BF16 = jnp.bfloat16
PEERS = 16
WORD = 256
VMEM = pl.BlockSpec(memory_space=pltpu.VMEM)
HBM = pl.BlockSpec(memory_space=pltpu.HBM)


def call(body, outs, args, flops=1 << 22, specs=None, out_specs=None, scratch=(), room=32):
    moved = sum(a.size * a.dtype.itemsize for a in args)
    return pl.pallas_call(
        body,
        out_shape=[jax.ShapeDtypeStruct(shape, dtype) for shape, dtype in outs],
        in_specs=specs or [VMEM] * len(args),
        out_specs=out_specs or [VMEM] * len(outs),
        scratch_shapes=scratch,
        compiler_params=pltpu.CompilerParams(vmem_limit_bytes=room << 20),
        cost_estimate=pl.CostEstimate(flops=flops, bytes_accessed=moved, transcendentals=0),
    )(*args)


def one_hot(ids, rows):
    grid = lax.broadcasted_iota(jnp.int32, (rows, ids.shape[1]), 0)
    return jnp.where(grid == ids, 1.0, 0.0).astype(BF16)


def mm(a, b):
    return lax.dot_general(a, b, (((1,), (0,)), ((), ())), preferred_element_type=F32)


def mm_t(a, b):
    return lax.dot_general(a, b, (((1,), (1,)), ((), ())), preferred_element_type=F32)


def core_of():
    return lax.axis_index("edge") & 1


def pieces(length):
    return [(at, min(WORD, length - at)) for at in range(0, length, WORD)]


def id_plan(edges, negatives):
    plan, row = [], 0
    for which, length, digits in ((0, edges, 2), (1, edges, 2), (2, edges, 1), (3, negatives, 1)):
        for digit in range(digits):
            plan.append((which, digit, row, length))
            row += len(pieces(length))
    return plan, -(-row // 32) * 32


def pack_kernel(block, src_ids, dst_ids, rel_ids, neg_ids, table, in_block, *scratch):
    held, sems, rows_f = scratch[:4], scratch[4], scratch[5]
    sources = (src_ids, dst_ids, rel_ids, neg_ids)
    copies = [pltpu.make_async_copy(block, in_block, sems.at[4])]
    for at, (source, target) in enumerate(zip(sources, held)):
        copies.append(pltpu.make_async_copy(source, target, sems.at[at]))
    for copy in copies:
        copy.start()
    for copy in copies[1:]:
        copy.wait()
    width = block.shape[0]
    plan, _ = id_plan(src_ids.shape[1], neg_ids.shape[1])
    rows_f[...] = jnp.full(rows_f.shape, -1.0, F32)
    for which, digit, row, length in plan:
        ids = held[which][...]
        ids = ids >> 8 if digit else ids & 255
        for step, (at, size) in enumerate(pieces(length)):
            rows_f[row + step : row + step + 1, :size] = ids[:, at : at + size].astype(F32)
    table[width:, :] = rows_f[...].astype(BF16)
    copies[0].wait()
    table[:width, :] = in_block[...].astype(BF16)


def unpack(table, width, edges, negatives):
    plan, _ = id_plan(edges, negatives)
    rows_f = table[width:, :].astype(F32)
    out = [None] * 4
    for which, digit, row, length in plan:
        parts = [
            rows_f[row + step : row + step + 1, : -(-size // 128) * 128]
            for step, (_, size) in enumerate(pieces(length))
        ]
        ids = jnp.concatenate(parts, axis=1).astype(jnp.int32)
        out[which] = out[which] + ids * 256 if digit else ids
    return out


def gather_kernel(
    negatives, own, hot, rel, block_s, hot_s, rel_s, src_out, rel_out, dst_out, hot_bf, rel_bf, states
):
    width, rows = hot.shape[0], own.shape[1]
    states[...] = jnp.zeros(states.shape, F32)
    for at, state in enumerate((block_s, hot_s, rel_s)):
        states[at : at + 1, : state.shape[1]] = state[...]
    hot_rows = hot.shape[1]
    src_at, dst_at, rel_at, _ = unpack(own, width, src_out.shape[1], negatives)
    hot_bf[...] = hot[...].astype(BF16)
    rel_bf[...] = rel[...].astype(BF16)
    src_out[...] = (
        mm(own[:width, :], one_hot(src_at, rows))
        + mm(hot_bf[...], one_hot(src_at - rows, hot_rows))
    ).astype(BF16)
    rel_out[...] = mm(rel_bf[...], one_hot(rel_at, rel.shape[1])).astype(BF16)
    dst_out[...] = mm(hot_bf[...], one_hot(dst_at - rows, hot_rows)).astype(BF16)


def edge_grads(partner, src, rel, dst, neg_at):
    query = (src * rel).astype(BF16)
    query_f = query.astype(F32)
    positive = jnp.sum(query_f * dst, axis=0, keepdims=True)
    pos_grad = -1.0 / (1.0 + jnp.exp(positive))
    scores = mm(partner.T, query)
    sig = (1.0 / (1.0 + jnp.exp(-scores))).astype(BF16)
    named = one_hot(neg_at, partner.shape[1])
    count = mm_t(jnp.ones((8, neg_at.shape[1]), BF16), named)[:1, :]
    scaled = partner.astype(F32) * count
    high = scaled.astype(BF16)
    low = (scaled - high.astype(F32)).astype(BF16)
    query_grad = pos_grad * dst + mm(high, sig) + mm(low, sig)
    src_grad = (query_grad * rel).astype(BF16)
    kind_grad = (query_grad * src).astype(BF16)
    dst_grad = (pos_grad * query_f).astype(BF16)
    return query, sig, count, src_grad, kind_grad, dst_grad


def grad_kernel(negatives, own, partner, hot, rel, src, rel_rows, dst_hot, keep, send):
    width, edges = src.shape
    rows, hot_rows = own.shape[1], hot.shape[1]
    half = rows // 2
    side = lax.axis_index("bucket") // (lax.axis_size("bucket") // 2)
    own_table, partner_table = own[:width, :], partner[:width, :]

    def hot_hits(at):
        return one_hot(at - rows - side * rows, rows)

    near_src, near_dst, near_rel, near_neg = unpack(own, width, edges, negatives)
    dst = mm(partner_table, one_hot(near_dst, rows)) + dst_hot[...].astype(F32)
    _, _, _, near_src_grad, near_kind_grad, near_dst_grad = edge_grads(
        partner_table, src[...].astype(F32), rel_rows[...].astype(F32), dst, near_neg
    )
    far_src, far_dst, far_rel, far_neg = unpack(partner, width, edges, negatives)
    ends = jnp.concatenate([far_src, far_dst], axis=1)
    from_hot = mm(hot[...], one_hot(ends - rows, hot_rows))
    src_rows = mm(partner_table, one_hot(far_src, rows)) + from_hot[:, :edges]
    dst_rows = mm(own_table, one_hot(far_dst, rows)) + from_hot[:, edges:]
    kind_rows = mm(rel[...], one_hot(far_rel, rel.shape[1]))
    query, sig, count, far_src_grad, far_kind_grad, far_dst_grad = edge_grads(
        own_table, src_rows, kind_rows, dst_rows, far_neg
    )
    cold = jnp.concatenate([near_src_grad, far_dst_grad], axis=1)
    cold_at = jnp.concatenate([near_src, far_dst], axis=1)
    block_sum = mm_t(query, sig) * count + mm_t(cold, one_hot(cold_at, rows))
    named = jnp.concatenate([near_dst_grad, cold, far_src_grad], axis=1)
    named_at = jnp.concatenate([near_dst, cold_at, far_src], axis=1)
    hot_sum = mm_t(named, hot_hits(named_at))
    kind_grad = jnp.concatenate([near_kind_grad, far_kind_grad], axis=1)
    kind_at = jnp.concatenate([near_rel, far_rel], axis=1)
    kind_sum = mm_t(kind_grad, one_hot(kind_at - side * half, half))

    @pl.when(core_of() == 0)
    def _():
        keep[:, :rows] = block_sum
        keep[:, rows:] = hot_sum
        send[:, :half] = kind_sum.astype(BF16)
        send[:, half:rows] = jnp.zeros((width, half), BF16)
        send[:, rows:] = hot_sum.astype(BF16)

    @pl.when(core_of() == 1)
    def _():
        keep[:, :half] = kind_sum
        keep[:, half:rows] = jnp.zeros((width, half), F32)
        keep[:, rows:] = hot_sum
        send[:, :rows] = block_sum.astype(BF16)
        send[:, rows:] = hot_sum.astype(BF16)


SIDES = (range(PEERS // 2), range(PEERS // 2, PEERS))
LANES = 128


def cuts(width):
    whole = width // PEERS
    last = width // (4 * PEERS)
    return whole, whole - last, last


def slot_rows(width):
    whole, near, last = cuts(width)
    sizes = (
        (2 * whole + 2 * near, 2 * whole + 2 * last),
        (2 * near, 4 * last),
        (2 * whole + 4 * near, 4 * whole + 4 * last),
    )
    return [-(-max(pair) // 8) * 8 for pair in sizes]


def merge_kernel(keep, got, out, sums, packed):
    width = keep.shape[0]
    whole, near, last = cuts(width)
    split = PEERS * near
    hot = slice(2 * LANES, 4 * LANES)

    def put(block, value):
        sums[block] = value

    def blank(end):
        if end < packed.shape[1]:
            packed[:, end:, :] = jnp.zeros((PEERS, packed.shape[1] - end, LANES), F32)

    for block in range(2):
        at = slice(hot.start + block * LANES, hot.start + (block + 1) * LANES)
        put(2 + block, keep[:, at] + got[:, at].astype(F32))

    @pl.when(core_of() == 0)
    def _():
        for block in range(2):
            at = slice(block * LANES, (block + 1) * LANES)
            put(block, keep[:, at] + got[:, at].astype(F32))
            for peer in range(PEERS):
                low = 2 * whole + block * near
                packed[peer, low : low + near, :] = sums[2 + block, peer * near : (peer + 1) * near, :]
        blank(2 * whole + 2 * near)

    @pl.when(core_of() == 1)
    def _():
        put(0, got[:, :LANES].astype(F32))
        put(1, keep[:, :LANES])
        for block in range(2):
            for peer in range(PEERS):
                low, start = 2 * whole + block * last, split + peer * last
                packed[peer, low : low + last, :] = sums[2 + block, start : start + last, :]
        blank(2 * whole + 2 * last)

    for block in range(2):
        for peer in range(PEERS):
            low = block * whole
            packed[peer, low : low + whole, :] = sums[block, peer * whole : (peer + 1) * whole, :]
    out[...] = packed[...].astype(BF16)


def peer_sum(ref, peers):
    total = ref[peers[0]].astype(F32)
    for peer in peers[1:]:
        total = total + ref[peer].astype(F32)
    return total


def first_kernel(width, got, out, held, total, row):
    whole, near, last = cuts(width)
    held[...] = jnp.zeros(held.shape, F32)
    row[...] = jnp.zeros(row.shape, F32)

    @pl.when(core_of() == 0)
    def _():
        total[...] = peer_sum(got, range(PEERS))
        held[: 2 * whole, :] = total[: 2 * whole, :]
        row[: 2 * near, :] = total[2 * whole : 2 * whole + 2 * near, :]

    @pl.when(core_of() == 1)
    def _():
        for side, peers in enumerate(SIDES):
            total[...] = peer_sum(got, peers)
            for core in range(2):
                at = (2 * core + side) * whole
                held[at : at + whole, :] = total[core * whole : (core + 1) * whole, :]
            at = side * 2 * last
            row[at : at + 2 * last, :] = total[2 * whole : 2 * whole + 2 * last, :]

    value = row[...].astype(BF16)
    for peer in range(PEERS):
        out[peer] = value


def second_kernel(width, got, held, out, total, row):
    whole, near, last = cuts(width)
    row[...] = jnp.zeros(row.shape, F32)

    @pl.when(core_of() == 0)
    def _():
        row[: 2 * whole, :] = held[: 2 * whole, :]
        for side, peers in enumerate(SIDES):
            total[...] = peer_sum(got, peers)
            at = 2 * whole + side * 2 * near
            row[at : at + 2 * near, :] = total[: 2 * near, :]

    @pl.when(core_of() == 1)
    def _():
        total[...] = peer_sum(got, range(PEERS))
        row[: 4 * whole, :] = held[: 4 * whole, :]
        row[4 * whole : 4 * whole + 4 * last, :] = total[: 4 * last, :]

    value = row[...].astype(BF16)
    for peer in range(PEERS):
        out[peer] = value


def update_kernel(mine, other, states, block, hot, rel, *refs):
    outs, state_outs, helds, state_held = refs[:3], refs[3:6], refs[6:9], refs[9]
    near_f, far_f, grads, sems = refs[10:]
    width, rows = block.shape
    whole, near, last = cuts(width)
    split = PEERS * near
    first = core_of() == 0
    copies = []
    state_held[...] = states[...]
    near_f[...] = jnp.where(first, mine[...], other[...]).astype(F32)
    far_f[...] = jnp.where(first, other[...], mine[...]).astype(F32)
    for table, weights in enumerate((block, hot, rel)):
        for column in range(weights.shape[1] // LANES):
            for peer in range(PEERS):
                at = slice(peer * whole, (peer + 1) * whole)
                low = column * whole
                if table == 0:
                    grads[at, :] = near_f[peer, low : low + whole, :]
                elif table == 2:
                    high = low + 2 * whole
                    grads[at, :] = jnp.where(
                        first, far_f[peer, low : low + whole, :], far_f[peer, high : high + whole, :]
                    )
                else:
                    low = 2 * whole + column * near
                    grads[peer * near : (peer + 1) * near, :] = near_f[peer, low : low + near, :]
                    low, start = 4 * whole + column * last, split + peer * last
                    grads[start : start + last, :] = far_f[peer, low : low + last, :]
            value = grads[...]
            at = slice(column * LANES, (column + 1) * LANES)
            total = states[table : table + 1, at] + jnp.sum(value * value, axis=0, keepdims=True) / width
            state_held[table : table + 1, at] = total
            helds[table][:, at] = weights[:, at] - value * (STEP / (jnp.sqrt(total) + EPS))
        state = state_held.at[table : table + 1, : weights.shape[1]]
        copies.append(pltpu.make_async_copy(helds[table], outs[table], sems.at[2 * table]))
        copies.append(pltpu.make_async_copy(state, state_outs[table], sems.at[2 * table + 1]))
        copies[-2].start()
        copies[-1].start()
    for copy in copies:
        copy.wait()


def flipped(x, axis, bit):
    return lax.ppermute(x, axis, [(i, i ^ bit) for i in range(lax.axis_size(axis))])


def exchanged(x, groups):
    return lax.all_to_all(x, ("bucket", "edge"), 0, 0, tiled=True, axis_index_groups=groups)


def edge_groups(core):
    n = lax.axis_size("edge")
    return [[b * n + e for e in range(core, n, 2)] for b in range(lax.axis_size("bucket"))]


def bucket_groups(core):
    n = lax.axis_size("edge")
    return [[b * n + e for b in range(lax.axis_size("bucket"))] for e in range(core, n, 2)]


def local(
    entity_block,
    block_state,
    hot_entities,
    hot_state,
    relations,
    relation_state,
    source_ids,
    target_ids,
    relation_ids,
    negative_ids,
):
    rows, width = entity_block.shape
    hot_rows = hot_entities.shape[0]
    edges = source_ids.shape[1]
    block_t, hot_t, rel_t = entity_block.T, hot_entities.T, relations.T
    negatives = negative_ids.shape[-1]
    ids = (source_ids, target_ids, relation_ids, negative_ids.reshape(1, -1))
    _, id_height = id_plan(edges, negatives)
    (own,) = call(
        pack_kernel,
        [((width + id_height, rows), BF16)],
        (block_t, *ids),
        specs=[HBM] * 5,
        room=63,
        scratch=[pltpu.VMEM((width, rows), F32)]
        + [pltpu.VMEM(part.shape, jnp.int32) for part in ids]
        + [pltpu.SemaphoreType.DMA((5,)), pltpu.VMEM((id_height, rows), F32)],
    )
    partner = flipped(own, "bucket", lax.axis_size("bucket") // 2)
    state_rows = [state.reshape(1, -1) for state in (block_state, hot_state, relation_state)]
    src, rel_rows, dst_hot, hot_bf, rel_bf, states = call(
        functools.partial(gather_kernel, negatives),
        [((width, edges), BF16)] * 3
        + [((width, hot_rows), BF16), ((width, rows), BF16), ((8, hot_rows), F32)],
        (own, hot_t, rel_t, *state_rows),
        1 << 30,
    )
    keep, send = call(
        functools.partial(grad_kernel, negatives),
        [((width, 2 * rows), F32), ((width, 2 * rows), BF16)],
        (own, partner, hot_bf, rel_bf, src, rel_rows, dst_hot),
        1 << 31,
    )
    both = edge_groups(0) + bucket_groups(1)
    sizes = slot_rows(width)
    whole = width // PEERS
    slots = [((PEERS, size, LANES), BF16) for size in sizes]
    rows_f = [pltpu.VMEM((size, LANES), F32) for size in sizes]
    (mixed,) = call(
        merge_kernel,
        [slots[0]],
        (keep, flipped(send, "edge", 1)),
        scratch=[pltpu.VMEM((4, width, LANES), F32), pltpu.VMEM((PEERS, sizes[0], LANES), F32)],
    )
    mixed = exchanged(mixed, both)
    hot_part, held = call(
        functools.partial(first_kernel, width),
        [slots[1], ((-(-4 * whole // 8) * 8, LANES), F32)],
        (mixed,),
        scratch=[rows_f[0], rows_f[1]],
    )
    hot_part = exchanged(hot_part, bucket_groups(0) + edge_groups(1))
    (totals,) = call(
        functools.partial(second_kernel, width),
        [slots[2]],
        (hot_part, held),
        scratch=[rows_f[1], rows_f[2]],
    )
    mine = exchanged(totals, both)
    other = flipped(mine, "edge", 1)
    tables = (block_t, hot_t, rel_t)
    new_block, new_hot, new_relations, *new_states = call(
        update_kernel,
        [(part.shape, F32) for part in (*tables, *state_rows)],
        (mine, other, states, *tables),
        out_specs=[HBM] * 6,
        scratch=[pltpu.VMEM(part.shape, F32) for part in (*tables, states, mine, mine)]
        + [pltpu.VMEM((width, LANES), F32), pltpu.SemaphoreType.DMA((6,))],
    )
    new_block_state, new_hot_state, new_relation_state = [part.reshape(-1) for part in new_states]
    return (
        new_block.T,
        new_block_state,
        new_hot.T,
        new_hot_state,
        new_relations.T,
        new_relation_state,
    )


def solution(mesh):
    placed = (
        P("bucket", None),
        P("bucket"),
        P(),
        P(),
        P("edge", None),
        P("edge"),
        P("bucket", "edge"),
        P("bucket", "edge"),
        P("bucket", "edge"),
        P("bucket", "edge", None),
    )
    return jax.shard_map(
        local,
        mesh=mesh,
        in_specs=placed,
        out_specs=(P("bucket", None), P("bucket"), P(), P(), P("edge", None), P("edge")),
        check_vma=False,
    )
```

```python
import functools

import jax
import jax.numpy as jnp
from jax import lax
from jax.experimental import pallas as pl
from jax.experimental.pallas import tpu as pltpu
from jax.sharding import PartitionSpec as P

STEP = 0.3
EPS = 1e-06
F32 = jnp.float32
BF16 = jnp.bfloat16
PEERS = 16
WORD = 256
VMEM = pl.BlockSpec(memory_space=pltpu.VMEM)
HBM = pl.BlockSpec(memory_space=pltpu.HBM)


def call(body, outs, args, flops=1 << 22, specs=None, out_specs=None, scratch=(), room=32, aliases=None):
    moved = sum(a.size * a.dtype.itemsize for a in args)
    return pl.pallas_call(
        body,
        out_shape=[jax.ShapeDtypeStruct(shape, dtype) for shape, dtype in outs],
        in_specs=specs or [VMEM] * len(args),
        out_specs=out_specs or [VMEM] * len(outs),
        scratch_shapes=scratch,
        input_output_aliases=aliases or {},
        compiler_params=pltpu.CompilerParams(vmem_limit_bytes=room << 20),
        cost_estimate=pl.CostEstimate(flops=flops, bytes_accessed=moved, transcendentals=0),
    )(*args)


def one_hot(ids, rows):
    grid = lax.broadcasted_iota(jnp.int16, (rows, ids.shape[1]), 0)
    return jnp.where(grid == ids.astype(jnp.int16), jnp.ones((), BF16), jnp.zeros((), BF16))


def mm(a, b):
    return lax.dot_general(a, b, (((1,), (0,)), ((), ())), preferred_element_type=F32)


def mm_t(a, b):
    return lax.dot_general(a, b, (((1,), (1,)), ((), ())), preferred_element_type=F32)


def core_of():
    return lax.axis_index("edge") & 1


def pieces(length):
    return [(at, min(WORD, length - at)) for at in range(0, length, WORD)]


def id_plan(edges, negatives):
    plan, row = [], 0
    for which, length, digits in ((0, edges, 2), (1, edges, 2), (2, edges, 1), (3, negatives, 1)):
        for digit in range(digits):
            plan.append((which, digit, row, length))
            row += len(pieces(length))
    return plan, -(-row // 32) * 32


def pack_kernel(block, src_ids, dst_ids, rel_ids, neg_ids, table, in_block, *scratch):
    held, sems, rows_f = scratch[:4], scratch[4], scratch[5]
    sources = (src_ids, dst_ids, rel_ids, neg_ids)
    copies = [pltpu.make_async_copy(block, in_block, sems.at[4])]
    for at, (source, target) in enumerate(zip(sources, held)):
        copies.append(pltpu.make_async_copy(source, target, sems.at[at]))
    for copy in copies:
        copy.start()
    for copy in copies[1:]:
        copy.wait()
    width = block.shape[0]
    plan, _ = id_plan(src_ids.shape[1], neg_ids.shape[1])
    rows_f[...] = jnp.full(rows_f.shape, -1.0, F32)
    for which, digit, row, length in plan:
        ids = held[which][...]
        ids = ids >> 8 if digit else ids & 255
        for step, (at, size) in enumerate(pieces(length)):
            rows_f[row + step : row + step + 1, :size] = ids[:, at : at + size].astype(F32)
    table[width:, :] = rows_f[...].astype(BF16)
    copies[0].wait()
    table[:width, :] = in_block[...].astype(BF16)


def unpack(table, width, edges, negatives):
    plan, _ = id_plan(edges, negatives)
    rows_f = table[width:, :].astype(F32)
    out = [None] * 4
    for which, digit, row, length in plan:
        parts = [
            rows_f[row + step : row + step + 1, : -(-size // 128) * 128]
            for step, (_, size) in enumerate(pieces(length))
        ]
        ids = jnp.concatenate(parts, axis=1).astype(jnp.int32)
        out[which] = out[which] + ids * 256 if digit else ids
    return out


def counts(neg_at, rows):
    ones = jnp.ones((8, neg_at.shape[1]), BF16)
    return mm_t(ones, one_hot(neg_at, rows))[:1, :]


def gather_kernel(
    negatives,
    own,
    hot,
    rel,
    block_s,
    hot_s,
    rel_s,
    src_out,
    rel_out,
    dst_out,
    query_out,
    hot_bf,
    rel_bf,
    states,
):
    width, rows = hot.shape[0], own.shape[1]
    states[...] = jnp.zeros(states.shape, F32)
    src_at, dst_at, rel_at, neg_at = unpack(own, width, src_out.shape[1], negatives)
    states[4:5, :rows] = counts(neg_at, rows)
    for at, state in enumerate((block_s, hot_s, rel_s)):
        states[at : at + 1, : state.shape[1]] = state[...]
    hot_rows = hot.shape[1]
    hot_bf[...] = hot[...].astype(BF16)
    rel_bf[...] = rel[...].astype(BF16)
    src_out[...] = (
        mm(own[:width, :], one_hot(src_at, rows))
        + mm(hot_bf[...], one_hot(src_at - rows, hot_rows))
    ).astype(BF16)
    rel_out[...] = mm(rel_bf[...], one_hot(rel_at, rel.shape[1])).astype(BF16)
    query_out[...] = (src_out[...].astype(F32) * rel_out[...].astype(F32)).astype(BF16)
    dst_out[...] = mm(hot_bf[...], one_hot(dst_at - rows, hot_rows)).astype(BF16)


def edge_grads(partner, src, rel, dst, query, count):
    query_f = query.astype(F32)
    positive = jnp.sum(query_f * dst, axis=0, keepdims=True)
    pos_grad = -1.0 / (1.0 + jnp.exp(positive))
    scores = mm(partner.T, query)
    sig = (1.0 / (1.0 + jnp.exp(-scores))).astype(BF16)
    weighed = (partner.astype(F32) * count).astype(BF16)
    query_grad = pos_grad * dst + mm(weighed, sig)
    src_grad = (query_grad * rel).astype(BF16)
    kind_grad = (query_grad * src).astype(BF16)
    dst_grad = (pos_grad * query_f).astype(BF16)
    return sig, src_grad, kind_grad, dst_grad


def grad_kernel(
    negatives, own, partner, hot, rel, src, rel_rows, dst_hot, near_query, states, keep, send
):
    width, edges = src.shape
    rows, hot_rows = own.shape[1], hot.shape[1]
    half = rows // 2
    side = lax.axis_index("bucket") // (lax.axis_size("bucket") // 2)
    own_table, partner_table = own[:width, :], partner[:width, :]

    def hot_hits(at):
        return one_hot(at - rows - side * rows, rows)

    near_src, near_dst, near_rel, _ = unpack(own, width, edges, negatives)
    dst = mm(partner_table, one_hot(near_dst, rows)) + dst_hot[...].astype(F32)
    _, near_src_grad, near_kind_grad, near_dst_grad = edge_grads(
        partner_table,
        src[...].astype(F32),
        rel_rows[...].astype(F32),
        dst,
        near_query[...],
        states[4:5, :rows],
    )
    far_src, far_dst, far_rel, far_neg = unpack(partner, width, edges, negatives)
    ends = jnp.concatenate([far_src, far_dst], axis=1)
    from_hot = mm(hot[...], one_hot(ends - rows, hot_rows))
    src_rows = mm(partner_table, one_hot(far_src, rows)) + from_hot[:, :edges]
    dst_rows = mm(own_table, one_hot(far_dst, rows)) + from_hot[:, edges:]
    kind_rows = mm(rel[...], one_hot(far_rel, rel.shape[1]))
    query = (src_rows * kind_rows).astype(BF16)
    count = counts(far_neg, rows)
    sig, far_src_grad, far_kind_grad, far_dst_grad = edge_grads(
        own_table, src_rows, kind_rows, dst_rows, query, count
    )
    cold = jnp.concatenate([near_src_grad, far_dst_grad], axis=1)
    cold_at = jnp.concatenate([near_src, far_dst], axis=1)
    block_sum = mm_t(query, sig) * count + mm_t(cold, one_hot(cold_at, rows))
    named = jnp.concatenate([near_dst_grad, cold, far_src_grad], axis=1)
    named_at = jnp.concatenate([near_dst, cold_at, far_src], axis=1)
    hot_sum = mm_t(named, hot_hits(named_at))
    kind_grad = jnp.concatenate([near_kind_grad, far_kind_grad], axis=1)
    kind_at = jnp.concatenate([near_rel, far_rel], axis=1)
    kind_sum = mm_t(kind_grad, one_hot(kind_at - side * half, half))

    @pl.when(core_of() == 0)
    def _():
        keep[:, :rows] = block_sum
        keep[:, rows:] = hot_sum
        send[:, :half] = kind_sum.astype(BF16)
        send[:, half:rows] = jnp.zeros((width, half), BF16)
        send[:, rows:] = hot_sum.astype(BF16)

    @pl.when(core_of() == 1)
    def _():
        keep[:, :half] = kind_sum
        keep[:, half:rows] = jnp.zeros((width, half), F32)
        keep[:, rows:] = hot_sum
        send[:, :rows] = block_sum.astype(BF16)
        send[:, rows:] = hot_sum.astype(BF16)


SIDES = (range(PEERS // 2), range(PEERS // 2, PEERS))
LANES = 128


def cuts(width):
    whole = width // PEERS
    last = width // (4 * PEERS)
    return whole, whole - last, last


def slot_rows(width):
    whole, near, last = cuts(width)
    sizes = (
        (2 * whole + 2 * near, 2 * whole + 2 * last),
        (2 * near, 4 * last),
        (2 * whole + 4 * near, 4 * whole + 4 * last),
    )
    return [-(-max(pair) // 8) * 8 for pair in sizes]


def merge_kernel(keep, got, out, sums, packed):
    width = keep.shape[0]
    whole, near, last = cuts(width)
    split = PEERS * near
    hot = slice(2 * LANES, 4 * LANES)

    def put(block, value):
        sums[block] = value

    def blank(end):
        if end < packed.shape[1]:
            packed[:, end:, :] = jnp.zeros((PEERS, packed.shape[1] - end, LANES), F32)

    for block in range(2):
        at = slice(hot.start + block * LANES, hot.start + (block + 1) * LANES)
        put(2 + block, keep[:, at] + got[:, at].astype(F32))

    @pl.when(core_of() == 0)
    def _():
        for block in range(2):
            at = slice(block * LANES, (block + 1) * LANES)
            put(block, keep[:, at] + got[:, at].astype(F32))
            for peer in range(PEERS):
                low = 2 * whole + block * near
                packed[peer, low : low + near, :] = sums[2 + block, peer * near : (peer + 1) * near, :]
        blank(2 * whole + 2 * near)

    @pl.when(core_of() == 1)
    def _():
        put(0, got[:, :LANES].astype(F32))
        put(1, keep[:, :LANES])
        for block in range(2):
            for peer in range(PEERS):
                low, start = 2 * whole + block * last, split + peer * last
                packed[peer, low : low + last, :] = sums[2 + block, start : start + last, :]
        blank(2 * whole + 2 * last)

    for block in range(2):
        for peer in range(PEERS):
            low = block * whole
            packed[peer, low : low + whole, :] = sums[block, peer * whole : (peer + 1) * whole, :]
    out[...] = packed[...].astype(BF16)


def peer_sum(ref, peers):
    total = ref[peers[0]].astype(F32)
    for peer in peers[1:]:
        total = total + ref[peer].astype(F32)
    return total


def first_kernel(width, got, out, held, total, row):
    whole, near, last = cuts(width)
    held[...] = jnp.zeros(held.shape, F32)
    row[...] = jnp.zeros(row.shape, F32)

    @pl.when(core_of() == 0)
    def _():
        total[...] = peer_sum(got, range(PEERS))
        held[: 2 * whole, :] = total[: 2 * whole, :]
        row[: 2 * near, :] = total[2 * whole : 2 * whole + 2 * near, :]

    @pl.when(core_of() == 1)
    def _():
        for side, peers in enumerate(SIDES):
            total[...] = peer_sum(got, peers)
            for core in range(2):
                at = (2 * core + side) * whole
                held[at : at + whole, :] = total[core * whole : (core + 1) * whole, :]
            at = side * 2 * last
            row[at : at + 2 * last, :] = total[2 * whole : 2 * whole + 2 * last, :]

    value = row[...].astype(BF16)
    for peer in range(PEERS):
        out[peer] = value


def second_kernel(width, got, held, out, total, row):
    whole, near, last = cuts(width)
    row[...] = jnp.zeros(row.shape, F32)

    @pl.when(core_of() == 0)
    def _():
        row[: 2 * whole, :] = held[: 2 * whole, :]
        for side, peers in enumerate(SIDES):
            total[...] = peer_sum(got, peers)
            at = 2 * whole + side * 2 * near
            row[at : at + 2 * near, :] = total[: 2 * near, :]

    @pl.when(core_of() == 1)
    def _():
        total[...] = peer_sum(got, range(PEERS))
        row[: 4 * whole, :] = held[: 4 * whole, :]
        row[4 * whole : 4 * whole + 4 * last, :] = total[: 4 * last, :]

    value = row[...].astype(BF16)
    for peer in range(PEERS):
        out[peer] = value


def stepped(table, column, grads, weights, states, held, state_held):
    at = slice(column * LANES, (column + 1) * LANES)
    total = jnp.sum(grads * grads, axis=0, keepdims=True) / grads.shape[0]
    total = states[table : table + 1, at] + total
    state_held[table : table + 1, at] = total
    held[:, at] = weights[:, at] - grads * (STEP / (jnp.sqrt(total) + EPS))


def written(table, held, state_held, out, state_out, sems):
    state = state_held.at[table : table + 1, : held.shape[1]]
    copies = [
        pltpu.make_async_copy(held, out, sems.at[2 * table]),
        pltpu.make_async_copy(state, state_out, sems.at[2 * table + 1]),
    ]
    for copy in copies:
        copy.start()
    return copies


def near_hot(rows_f, hot_rows, whole, near):
    for column in range(hot_rows.shape[0]):
        for peer in range(PEERS):
            low = 2 * whole + column * near
            hot_rows[column, peer * near : (peer + 1) * near, :] = rows_f[peer, low : low + near, :]


def last_hot(rows_f, hot_rows, whole, near, last):
    for column in range(hot_rows.shape[0]):
        for peer in range(PEERS):
            low, start = 4 * whole + column * last, PEERS * near + peer * last
            hot_rows[column, start : start + last, :] = rows_f[peer, low : low + last, :]


def whole_rows(rows_f, grads, whole, low):
    for peer in range(PEERS):
        grads[peer * whole : (peer + 1) * whole, :] = rows_f[peer, low : low + whole, :]
    return grads[...]


def early_kernel(
    mine, states, block, rel, new_b, new_bs, new_r, new_rs, hot_rows, rows_f, held, state_held, grads, sems
):
    whole, near, last = cuts(block.shape[0])
    rows_f[...] = mine[...].astype(F32)

    @pl.when(core_of() == 0)
    def _():
        for column in range(2):
            value = whole_rows(rows_f, grads, whole, column * whole)
            stepped(0, column, value, block, states, held, state_held)
        copies = written(0, held, state_held, new_b, new_bs, sems)
        near_hot(rows_f, hot_rows, whole, near)
        for copy in copies:
            copy.wait()

    @pl.when(core_of() == 1)
    def _():
        for column in range(2):
            value = whole_rows(rows_f, grads, whole, (2 + column) * whole)
            stepped(2, column, value, rel, states, held, state_held)
        copies = written(2, held, state_held, new_r, new_rs, sems)
        last_hot(rows_f, hot_rows, whole, near, last)
        for copy in copies:
            copy.wait()


def late_kernel(
    other, states, block, hot, rel, part, in_b, in_bs, in_r, in_rs, new_b, new_bs, new_r, new_rs, new_h, new_hs, *refs
):
    del in_b, in_bs, in_r, in_rs
    rows_f, hot_rows, held_hot, held, state_held, grads, sems = refs
    width = block.shape[0]
    whole, near, last = cuts(width)
    split = PEERS * near
    rows_f[...] = other[...].astype(F32)

    def hot_steps():
        for column in range(hot_rows.shape[0]):
            stepped(1, column, hot_rows[column], hot, states, held_hot, state_held)
        return written(1, held_hot, state_held, new_h, new_hs, sems)

    @pl.when(core_of() == 0)
    def _():
        hot_rows[:, :split, :] = part[:, :split, :]
        last_hot(rows_f, hot_rows, whole, near, last)
        copies = hot_steps()
        for column in range(2):
            value = whole_rows(rows_f, grads, whole, column * whole)
            stepped(2, column, value, rel, states, held, state_held)
        for copy in copies + written(2, held, state_held, new_r, new_rs, sems):
            copy.wait()

    @pl.when(core_of() == 1)
    def _():
        hot_rows[:, split:, :] = part[:, split:, :]
        near_hot(rows_f, hot_rows, whole, near)
        copies = hot_steps()
        for column in range(2):
            value = whole_rows(rows_f, grads, whole, column * whole)
            stepped(0, column, value, block, states, held, state_held)
        for copy in copies + written(0, held, state_held, new_b, new_bs, sems):
            copy.wait()


def flipped(x, axis, bit):
    return lax.ppermute(x, axis, [(i, i ^ bit) for i in range(lax.axis_size(axis))])


def exchanged(x, groups):
    return lax.all_to_all(x, ("bucket", "edge"), 0, 0, tiled=True, axis_index_groups=groups)


def edge_groups(core):
    n = lax.axis_size("edge")
    return [[b * n + e for e in range(core, n, 2)] for b in range(lax.axis_size("bucket"))]


def bucket_groups(core):
    n = lax.axis_size("edge")
    return [[b * n + e for b in range(lax.axis_size("bucket"))] for e in range(core, n, 2)]


def local(
    entity_block,
    block_state,
    hot_entities,
    hot_state,
    relations,
    relation_state,
    source_ids,
    target_ids,
    relation_ids,
    negative_ids,
):
    rows, width = entity_block.shape
    hot_rows = hot_entities.shape[0]
    edges = source_ids.shape[1]
    block_t, hot_t, rel_t = entity_block.T, hot_entities.T, relations.T
    negatives = negative_ids.shape[-1]
    ids = (source_ids, target_ids, relation_ids, negative_ids.reshape(1, -1))
    _, id_height = id_plan(edges, negatives)
    (own,) = call(
        pack_kernel,
        [((width + id_height, rows), BF16)],
        (block_t, *ids),
        specs=[HBM] * 5,
        room=63,
        scratch=[pltpu.VMEM((width, rows), F32)]
        + [pltpu.VMEM(part.shape, jnp.int32) for part in ids]
        + [pltpu.SemaphoreType.DMA((5,)), pltpu.VMEM((id_height, rows), F32)],
    )
    partner = flipped(own, "bucket", lax.axis_size("bucket") // 2)
    state_rows = [state.reshape(1, -1) for state in (block_state, hot_state, relation_state)]
    src, rel_rows, dst_hot, near_query, hot_bf, rel_bf, states = call(
        functools.partial(gather_kernel, negatives),
        [((width, edges), BF16)] * 4
        + [((width, hot_rows), BF16), ((width, rows), BF16), ((8, hot_rows), F32)],
        (own, hot_t, rel_t, *state_rows),
        1 << 30,
    )
    keep, send = call(
        functools.partial(grad_kernel, negatives),
        [((width, 2 * rows), F32), ((width, 2 * rows), BF16)],
        (own, partner, hot_bf, rel_bf, src, rel_rows, dst_hot, near_query, states),
        1 << 31,
    )
    both = edge_groups(0) + bucket_groups(1)
    sizes = slot_rows(width)
    whole = width // PEERS
    slots = [((PEERS, size, LANES), BF16) for size in sizes]
    rows_f = [pltpu.VMEM((size, LANES), F32) for size in sizes]
    (mixed,) = call(
        merge_kernel,
        [slots[0]],
        (keep, flipped(send, "edge", 1)),
        scratch=[pltpu.VMEM((4, width, LANES), F32), pltpu.VMEM((PEERS, sizes[0], LANES), F32)],
    )
    mixed = exchanged(mixed, both)
    hot_part, held = call(
        functools.partial(first_kernel, width),
        [slots[1], ((-(-4 * whole // 8) * 8, LANES), F32)],
        (mixed,),
        scratch=[rows_f[0], rows_f[1]],
    )
    hot_part = exchanged(hot_part, bucket_groups(0) + edge_groups(1))
    (totals,) = call(
        functools.partial(second_kernel, width),
        [slots[2]],
        (hot_part, held),
        scratch=[rows_f[1], rows_f[2]],
    )
    mine = exchanged(totals, both)
    other = flipped(mine, "edge", 1)
    block_s, hot_s, rel_s = [(part.shape, F32) for part in state_rows]
    block_like, hot_like = (block_t.shape, F32), (hot_t.shape, F32)
    columns = ((hot_rows // LANES, width, LANES), F32)
    held = [pltpu.VMEM(block_t.shape, F32), pltpu.VMEM(states.shape, F32)]
    held += [pltpu.VMEM((width, LANES), F32), pltpu.SemaphoreType.DMA((6,))]
    *done, part = call(
        early_kernel,
        [block_like, block_s, block_like, rel_s, columns],
        (mine, states, block_t, rel_t),
        out_specs=[HBM] * 4 + [VMEM],
        scratch=[pltpu.VMEM(mine.shape, F32)] + held,
    )
    new_block, new_block_state, new_relations, new_relation_state, new_hot, new_hot_state = call(
        late_kernel,
        [block_like, block_s, block_like, rel_s, hot_like, hot_s],
        (other, states, block_t, hot_t, rel_t, part, *done),
        specs=[VMEM] * 6 + [HBM] * 4,
        out_specs=[HBM] * 6,
        scratch=[pltpu.VMEM(mine.shape, F32), pltpu.VMEM(*columns), pltpu.VMEM(*hot_like)] + held,
        aliases={6 + at: at for at in range(4)},
    )
    new_block_state, new_hot_state, new_relation_state = [
        part.reshape(-1) for part in (new_block_state, new_hot_state, new_relation_state)
    ]
    return (
        new_block.T,
        new_block_state,
        new_hot.T,
        new_hot_state,
        new_relations.T,
        new_relation_state,
    )


def solution(mesh):
    placed = (
        P("bucket", None),
        P("bucket"),
        P(),
        P(),
        P("edge", None),
        P("edge"),
        P("bucket", "edge"),
        P("bucket", "edge"),
        P("bucket", "edge"),
        P("bucket", "edge", None),
    )
    return jax.shard_map(
        local,
        mesh=mesh,
        in_specs=placed,
        out_specs=(P("bucket", None), P("bucket"), P(), P(), P("edge", None), P("edge")),
        check_vma=False,
    )
```

```python
import functools

import jax
import jax.numpy as jnp
from jax import lax
from jax.experimental import pallas as pl
from jax.experimental.pallas import tpu as pltpu
from jax.sharding import PartitionSpec as P

STEP = 0.3
EPS = 1e-06
F32 = jnp.float32
BF16 = jnp.bfloat16
PEERS = 16
WORD = 256
VMEM = pl.BlockSpec(memory_space=pltpu.VMEM)
HBM = pl.BlockSpec(memory_space=pltpu.HBM)


def call(body, outs, args, flops=1 << 22, specs=None, out_specs=None, scratch=(), aliases=None):
    moved = sum(a.size * a.dtype.itemsize for a in args)
    return pl.pallas_call(
        body,
        out_shape=[jax.ShapeDtypeStruct(shape, dtype) for shape, dtype in outs],
        in_specs=specs or [VMEM] * len(args),
        out_specs=out_specs or [VMEM] * len(outs),
        scratch_shapes=scratch,
        input_output_aliases=aliases or {},
        compiler_params=pltpu.CompilerParams(vmem_limit_bytes=32 << 20),
        cost_estimate=pl.CostEstimate(flops=flops, bytes_accessed=moved, transcendentals=0),
    )(*args)


def one_hot(ids, rows):
    grid = lax.broadcasted_iota(jnp.int16, (rows, ids.shape[1]), 0)
    return jnp.where(grid == ids.astype(jnp.int16), jnp.ones((), BF16), jnp.zeros((), BF16))


def mm(a, b):
    return lax.dot_general(a, b, (((1,), (0,)), ((), ())), preferred_element_type=F32)


def mm_t(a, b):
    return lax.dot_general(a, b, (((1,), (1,)), ((), ())), preferred_element_type=F32)


def core_of():
    return lax.axis_index("edge") & 1


def pieces(length):
    return [(at, min(WORD, length - at)) for at in range(0, length, WORD)]


def id_plan(edges, negatives):
    plan, row = [], 0
    for which, length, digits in ((0, edges, 2), (1, edges, 2), (2, edges, 1), (3, negatives, 1)):
        for digit in range(digits):
            plan.append((which, digit, row, length))
            row += len(pieces(length))
    return plan, -(-row // 32) * 32


def pack_kernel(block, src_ids, dst_ids, rel_ids, neg_ids, table, in_block, *scratch):
    held, sems, rows_f = scratch[:4], scratch[4], scratch[5]
    sources = (src_ids, dst_ids, rel_ids, neg_ids)
    copies = [pltpu.make_async_copy(block, in_block, sems.at[4])]
    for at, (source, target) in enumerate(zip(sources, held)):
        copies.append(pltpu.make_async_copy(source, target, sems.at[at]))
    for copy in copies:
        copy.start()
    for copy in copies[1:]:
        copy.wait()
    width = block.shape[0]
    plan, _ = id_plan(src_ids.shape[1], neg_ids.shape[1])
    rows_f[...] = jnp.full(rows_f.shape, -1.0, F32)
    for which, digit, row, length in plan:
        ids = held[which][...]
        ids = ids >> 8 if digit else ids & 255
        for step, (at, size) in enumerate(pieces(length)):
            rows_f[row + step : row + step + 1, :size] = ids[:, at : at + size].astype(F32)
    table[width:, :] = rows_f[...].astype(BF16)
    copies[0].wait()
    table[:width, :] = in_block[...].astype(BF16)


def unpack(table, width, edges, negatives):
    plan, _ = id_plan(edges, negatives)
    rows_f = table[width:, :].astype(F32)
    out = [None] * 4
    for which, digit, row, length in plan:
        parts = [
            rows_f[row + step : row + step + 1, : -(-size // 128) * 128]
            for step, (_, size) in enumerate(pieces(length))
        ]
        ids = jnp.concatenate(parts, axis=1).astype(jnp.int32)
        out[which] = out[which] + ids * 256 if digit else ids
    return out


def counts(neg_at, rows):
    ones = jnp.ones((8, neg_at.shape[1]), BF16)
    return mm_t(ones, one_hot(neg_at, rows))[:1, :]


def gather_kernel(
    negatives,
    own,
    hot,
    rel,
    block_s,
    hot_s,
    rel_s,
    src_out,
    rel_out,
    dst_out,
    query_out,
    hot_bf,
    rel_bf,
    states,
):
    width, rows = hot.shape[0], own.shape[1]
    states[...] = jnp.zeros(states.shape, F32)
    src_at, dst_at, rel_at, neg_at = unpack(own, width, src_out.shape[1], negatives)
    states[4:5, :rows] = counts(neg_at, rows)
    for at, state in enumerate((block_s, hot_s, rel_s)):
        states[at : at + 1, : state.shape[1]] = state[...]
    hot_rows = hot.shape[1]
    hot_bf[...] = hot[...].astype(BF16)
    rel_bf[...] = rel[...].astype(BF16)
    src_out[...] = (
        mm(own[:width, :], one_hot(src_at, rows))
        + mm(hot_bf[...], one_hot(src_at - rows, hot_rows))
    ).astype(BF16)
    rel_out[...] = mm(rel_bf[...], one_hot(rel_at, rel.shape[1])).astype(BF16)
    query_out[...] = (src_out[...].astype(F32) * rel_out[...].astype(F32)).astype(BF16)
    dst_out[...] = mm(hot_bf[...], one_hot(dst_at - rows, hot_rows)).astype(BF16)


def edge_grads(partner, src, rel, dst, query, count):
    query_f = query.astype(F32)
    positive = jnp.sum(query_f * dst, axis=0, keepdims=True)
    pos_grad = -1.0 / (1.0 + jnp.exp(positive))
    scores = mm(partner.T, query)
    sig = (1.0 / (1.0 + jnp.exp(-scores))).astype(BF16)
    weighed = (partner.astype(F32) * count).astype(BF16)
    query_grad = pos_grad * dst + mm(weighed, sig)
    src_grad = (query_grad * rel).astype(BF16)
    kind_grad = (query_grad * src).astype(BF16)
    dst_grad = (pos_grad * query_f).astype(BF16)
    return sig, src_grad, kind_grad, dst_grad


def grad_kernel(
    negatives, own, partner, hot, rel, src, rel_rows, dst_hot, near_query, states, keep, send
):
    width, edges = src.shape
    rows, hot_rows = own.shape[1], hot.shape[1]
    half = rows // 2
    side = lax.axis_index("bucket") // (lax.axis_size("bucket") // 2)
    own_table, partner_table = own[:width, :], partner[:width, :]

    def hot_hits(at):
        return one_hot(at - rows - side * rows, rows)

    near_src, near_dst, near_rel, _ = unpack(own, width, edges, negatives)
    dst = mm(partner_table, one_hot(near_dst, rows)) + dst_hot[...].astype(F32)
    _, near_src_grad, near_kind_grad, near_dst_grad = edge_grads(
        partner_table,
        src[...].astype(F32),
        rel_rows[...].astype(F32),
        dst,
        near_query[...],
        states[4:5, :rows],
    )
    far_src, far_dst, far_rel, far_neg = unpack(partner, width, edges, negatives)
    ends = jnp.concatenate([far_src, far_dst], axis=1)
    from_hot = mm(hot[...], one_hot(ends - rows, hot_rows))
    src_rows = mm(partner_table, one_hot(far_src, rows)) + from_hot[:, :edges]
    dst_rows = mm(own_table, one_hot(far_dst, rows)) + from_hot[:, edges:]
    kind_rows = mm(rel[...], one_hot(far_rel, rel.shape[1]))
    query = (src_rows * kind_rows).astype(BF16)
    count = counts(far_neg, rows)
    sig, far_src_grad, far_kind_grad, far_dst_grad = edge_grads(
        own_table, src_rows, kind_rows, dst_rows, query, count
    )
    cold = jnp.concatenate([near_src_grad, far_dst_grad], axis=1)
    cold_at = jnp.concatenate([near_src, far_dst], axis=1)
    block_sum = mm_t(query, sig) * count + mm_t(cold, one_hot(cold_at, rows))
    named = jnp.concatenate([near_dst_grad, cold, far_src_grad], axis=1)
    named_at = jnp.concatenate([near_dst, cold_at, far_src], axis=1)
    hot_sum = mm_t(named, hot_hits(named_at))
    kind_grad = jnp.concatenate([near_kind_grad, far_kind_grad], axis=1)
    kind_at = jnp.concatenate([near_rel, far_rel], axis=1)
    kind_sum = mm_t(kind_grad, one_hot(kind_at - side * half, half))

    @pl.when(core_of() == 0)
    def _():
        keep[:, :rows] = block_sum
        keep[:, rows:] = hot_sum
        send[:, :half] = kind_sum.astype(BF16)
        send[:, half:rows] = jnp.zeros((width, half), BF16)
        send[:, rows:] = hot_sum.astype(BF16)

    @pl.when(core_of() == 1)
    def _():
        keep[:, :half] = kind_sum
        keep[:, half:rows] = jnp.zeros((width, half), F32)
        keep[:, rows:] = hot_sum
        send[:, :rows] = block_sum.astype(BF16)
        send[:, rows:] = hot_sum.astype(BF16)


SIDES = (range(PEERS // 2), range(PEERS // 2, PEERS))
LANES = 128


def cuts(width):
    whole = width // PEERS
    last = width // (4 * PEERS)
    return whole, whole - last, last


def slot_rows(width):
    whole, near, last = cuts(width)
    sizes = (
        (2 * whole + 2 * near, 2 * whole + 2 * last),
        (2 * near, 4 * last),
        (2 * whole + 4 * near, 4 * whole + 4 * last),
    )
    return [-(-max(pair) // 8) * 8 for pair in sizes]


def merge_kernel(keep, got, out, sums, packed):
    width = keep.shape[0]
    whole, near, last = cuts(width)
    split = PEERS * near
    hot = slice(2 * LANES, 4 * LANES)

    def put(block, value):
        sums[block] = value

    def blank(end):
        if end < packed.shape[1]:
            packed[:, end:, :] = jnp.zeros((PEERS, packed.shape[1] - end, LANES), F32)

    for block in range(2):
        at = slice(hot.start + block * LANES, hot.start + (block + 1) * LANES)
        put(2 + block, keep[:, at] + got[:, at].astype(F32))

    @pl.when(core_of() == 0)
    def _():
        for block in range(2):
            at = slice(block * LANES, (block + 1) * LANES)
            put(block, keep[:, at] + got[:, at].astype(F32))
            for peer in range(PEERS):
                low = 2 * whole + block * near
                packed[peer, low : low + near, :] = sums[2 + block, peer * near : (peer + 1) * near, :]
        blank(2 * whole + 2 * near)

    @pl.when(core_of() == 1)
    def _():
        put(0, got[:, :LANES].astype(F32))
        put(1, keep[:, :LANES])
        for block in range(2):
            for peer in range(PEERS):
                low, start = 2 * whole + block * last, split + peer * last
                packed[peer, low : low + last, :] = sums[2 + block, start : start + last, :]
        blank(2 * whole + 2 * last)

    for block in range(2):
        for peer in range(PEERS):
            low = block * whole
            packed[peer, low : low + whole, :] = sums[block, peer * whole : (peer + 1) * whole, :]
    out[...] = packed[...].astype(BF16)


def peer_sum(ref, peers):
    total = ref[peers[0]].astype(F32)
    for peer in peers[1:]:
        total = total + ref[peer].astype(F32)
    return total


def first_kernel(width, got, out, held, total, row):
    whole, near, last = cuts(width)
    held[...] = jnp.zeros(held.shape, F32)
    row[...] = jnp.zeros(row.shape, F32)

    @pl.when(core_of() == 0)
    def _():
        total[...] = peer_sum(got, range(PEERS))
        held[: 2 * whole, :] = total[: 2 * whole, :]
        row[: 2 * near, :] = total[2 * whole : 2 * whole + 2 * near, :]

    @pl.when(core_of() == 1)
    def _():
        for side, peers in enumerate(SIDES):
            total[...] = peer_sum(got, peers)
            for core in range(2):
                at = (2 * core + side) * whole
                held[at : at + whole, :] = total[core * whole : (core + 1) * whole, :]
            at = side * 2 * last
            row[at : at + 2 * last, :] = total[2 * whole : 2 * whole + 2 * last, :]

    value = row[...].astype(BF16)
    for peer in range(PEERS):
        out[peer] = value


def second_kernel(width, got, held, out, total, row):
    whole, near, last = cuts(width)
    row[...] = jnp.zeros(row.shape, F32)

    @pl.when(core_of() == 0)
    def _():
        row[: 2 * whole, :] = held[: 2 * whole, :]
        for side, peers in enumerate(SIDES):
            total[...] = peer_sum(got, peers)
            at = 2 * whole + side * 2 * near
            row[at : at + 2 * near, :] = total[: 2 * near, :]

    @pl.when(core_of() == 1)
    def _():
        total[...] = peer_sum(got, range(PEERS))
        row[: 4 * whole, :] = held[: 4 * whole, :]
        row[4 * whole : 4 * whole + 4 * last, :] = total[: 4 * last, :]

    value = row[...].astype(BF16)
    for peer in range(PEERS):
        out[peer] = value


def stepped(table, column, grads, weights, states, held, state_held):
    at = slice(column * LANES, (column + 1) * LANES)
    total = jnp.sum(grads * grads, axis=0, keepdims=True) / grads.shape[0]
    total = states[table : table + 1, at] + total
    state_held[table : table + 1, at] = total
    held[:, at] = weights[:, at] - grads * (STEP / (jnp.sqrt(total) + EPS))


def written(table, held, state_held, out, state_out, sems):
    state = state_held.at[table : table + 1, : held.shape[1]]
    copies = [
        pltpu.make_async_copy(held, out, sems.at[2 * table]),
        pltpu.make_async_copy(state, state_out, sems.at[2 * table + 1]),
    ]
    for copy in copies:
        copy.start()
    return copies


def near_hot(rows_f, hot_rows, whole, near):
    for column in range(hot_rows.shape[0]):
        for peer in range(PEERS):
            low = 2 * whole + column * near
            hot_rows[column, peer * near : (peer + 1) * near, :] = rows_f[peer, low : low + near, :]


def last_hot(rows_f, hot_rows, whole, near, last):
    for column in range(hot_rows.shape[0]):
        for peer in range(PEERS):
            low, start = 4 * whole + column * last, PEERS * near + peer * last
            hot_rows[column, start : start + last, :] = rows_f[peer, low : low + last, :]


def whole_rows(rows_f, grads, whole, low):
    for peer in range(PEERS):
        grads[peer * whole : (peer + 1) * whole, :] = rows_f[peer, low : low + whole, :]
    return grads[...]


def early_kernel(
    mine, states, block, rel, new_b, new_bs, new_r, new_rs, hot_rows, rows_f, held, state_held, grads, sems
):
    whole, near, last = cuts(block.shape[0])
    rows_f[...] = mine[...].astype(F32)

    @pl.when(core_of() == 0)
    def _():
        for column in range(2):
            value = whole_rows(rows_f, grads, whole, column * whole)
            stepped(0, column, value, block, states, held, state_held)
        copies = written(0, held, state_held, new_b, new_bs, sems)
        near_hot(rows_f, hot_rows, whole, near)
        for copy in copies:
            copy.wait()

    @pl.when(core_of() == 1)
    def _():
        for column in range(2):
            value = whole_rows(rows_f, grads, whole, (2 + column) * whole)
            stepped(2, column, value, rel, states, held, state_held)
        copies = written(2, held, state_held, new_r, new_rs, sems)
        last_hot(rows_f, hot_rows, whole, near, last)
        for copy in copies:
            copy.wait()


def late_kernel(
    other, states, block, hot, rel, part, in_b, in_bs, in_r, in_rs, new_b, new_bs, new_r, new_rs, new_h, new_hs, *refs
):
    del in_b, in_bs, in_r, in_rs
    rows_f, hot_rows, held_hot, held, state_held, grads, sems = refs
    width = block.shape[0]
    whole, near, last = cuts(width)
    split = PEERS * near
    rows_f[...] = other[...].astype(F32)

    def hot_steps():
        for column in range(hot_rows.shape[0]):
            stepped(1, column, hot_rows[column], hot, states, held_hot, state_held)
        return written(1, held_hot, state_held, new_h, new_hs, sems)

    @pl.when(core_of() == 0)
    def _():
        hot_rows[:, :split, :] = part[:, :split, :]
        last_hot(rows_f, hot_rows, whole, near, last)
        copies = hot_steps()
        for column in range(2):
            value = whole_rows(rows_f, grads, whole, column * whole)
            stepped(2, column, value, rel, states, held, state_held)
        for copy in copies + written(2, held, state_held, new_r, new_rs, sems):
            copy.wait()

    @pl.when(core_of() == 1)
    def _():
        hot_rows[:, split:, :] = part[:, split:, :]
        near_hot(rows_f, hot_rows, whole, near)
        copies = hot_steps()
        for column in range(2):
            value = whole_rows(rows_f, grads, whole, column * whole)
            stepped(0, column, value, block, states, held, state_held)
        for copy in copies + written(0, held, state_held, new_b, new_bs, sems):
            copy.wait()


def flipped(x, axis, bit):
    return lax.ppermute(x, axis, [(i, i ^ bit) for i in range(lax.axis_size(axis))])


def exchanged(x, groups):
    return lax.all_to_all(x, ("bucket", "edge"), 0, 0, tiled=True, axis_index_groups=groups)


def edge_groups(core):
    n = lax.axis_size("edge")
    return [[b * n + e for e in range(core, n, 2)] for b in range(lax.axis_size("bucket"))]


def bucket_groups(core):
    n = lax.axis_size("edge")
    return [[b * n + e for b in range(lax.axis_size("bucket"))] for e in range(core, n, 2)]


def local(
    entity_block,
    block_state,
    hot_entities,
    hot_state,
    relations,
    relation_state,
    source_ids,
    target_ids,
    relation_ids,
    negative_ids,
):
    rows, width = entity_block.shape
    hot_rows = hot_entities.shape[0]
    edges = source_ids.shape[1]
    block_t, hot_t, rel_t = entity_block.T, hot_entities.T, relations.T
    negatives = negative_ids.shape[-1]
    ids = (source_ids, target_ids, relation_ids, negative_ids.reshape(1, -1))
    _, id_height = id_plan(edges, negatives)
    (own,) = call(
        pack_kernel,
        [((width + id_height, rows), BF16)],
        [pltpu.with_memory_space_constraint(part, pltpu.HBM) for part in (block_t, *ids)],
        specs=[HBM] * 5,
        scratch=[pltpu.VMEM((width, rows), F32)]
        + [pltpu.VMEM(part.shape, jnp.int32) for part in ids]
        + [pltpu.SemaphoreType.DMA((5,)), pltpu.VMEM((id_height, rows), F32)],
    )
    partner = flipped(own, "bucket", lax.axis_size("bucket") // 2)
    state_rows = [state.reshape(1, -1) for state in (block_state, hot_state, relation_state)]
    src, rel_rows, dst_hot, near_query, hot_bf, rel_bf, states = call(
        functools.partial(gather_kernel, negatives),
        [((width, edges), BF16)] * 4
        + [((width, hot_rows), BF16), ((width, rows), BF16), ((8, hot_rows), F32)],
        (own, hot_t, rel_t, *state_rows),
        1 << 30,
    )
    keep, send = call(
        functools.partial(grad_kernel, negatives),
        [((width, 2 * rows), F32), ((width, 2 * rows), BF16)],
        (own, partner, hot_bf, rel_bf, src, rel_rows, dst_hot, near_query, states),
        1 << 31,
    )
    both = edge_groups(0) + bucket_groups(1)
    sizes = slot_rows(width)
    whole = width // PEERS
    slots = [((PEERS, size, LANES), BF16) for size in sizes]
    rows_f = [pltpu.VMEM((size, LANES), F32) for size in sizes]
    (mixed,) = call(
        merge_kernel,
        [slots[0]],
        (keep, flipped(send, "edge", 1)),
        scratch=[pltpu.VMEM((4, width, LANES), F32), pltpu.VMEM((PEERS, sizes[0], LANES), F32)],
    )
    mixed = exchanged(mixed, both)
    hot_part, held = call(
        functools.partial(first_kernel, width),
        [slots[1], ((-(-4 * whole // 8) * 8, LANES), F32)],
        (mixed,),
        scratch=[rows_f[0], rows_f[1]],
    )
    hot_part = exchanged(hot_part, bucket_groups(0) + edge_groups(1))
    (totals,) = call(
        functools.partial(second_kernel, width),
        [slots[2]],
        (hot_part, held),
        scratch=[rows_f[1], rows_f[2]],
    )
    mine = exchanged(totals, both)
    other = flipped(mine, "edge", 1)
    block_s, hot_s, rel_s = [(part.shape, F32) for part in state_rows]
    block_like, hot_like = (block_t.shape, F32), (hot_t.shape, F32)
    columns = ((hot_rows // LANES, width, LANES), F32)
    held = [pltpu.VMEM(block_t.shape, F32), pltpu.VMEM(states.shape, F32)]
    held += [pltpu.VMEM((width, LANES), F32), pltpu.SemaphoreType.DMA((6,))]
    *done, part = call(
        early_kernel,
        [block_like, block_s, block_like, rel_s, columns],
        (mine, states, block_t, rel_t),
        out_specs=[HBM] * 4 + [VMEM],
        scratch=[pltpu.VMEM(mine.shape, F32)] + held,
    )
    new_block, new_block_state, new_relations, new_relation_state, new_hot, new_hot_state = call(
        late_kernel,
        [block_like, block_s, block_like, rel_s, hot_like, hot_s],
        (other, states, block_t, hot_t, rel_t, part, *done),
        specs=[VMEM] * 6 + [HBM] * 4,
        out_specs=[HBM] * 6,
        scratch=[pltpu.VMEM(mine.shape, F32), pltpu.VMEM(*columns), pltpu.VMEM(*hot_like)] + held,
        aliases={6 + at: at for at in range(4)},
    )
    new_block_state, new_hot_state, new_relation_state = [
        part.reshape(-1) for part in (new_block_state, new_hot_state, new_relation_state)
    ]
    return (
        new_block.T,
        new_block_state,
        new_hot.T,
        new_hot_state,
        new_relations.T,
        new_relation_state,
    )


def solution(mesh):
    placed = (
        P("bucket", None),
        P("bucket"),
        P(),
        P(),
        P("edge", None),
        P("edge"),
        P("bucket", "edge"),
        P("bucket", "edge"),
        P("bucket", "edge"),
        P("bucket", "edge", None),
    )
    return jax.shard_map(
        local,
        mesh=mesh,
        in_specs=placed,
        out_specs=(P("bucket", None), P("bucket"), P(), P(), P("edge", None), P("edge")),
        check_vma=False,
    )
```

```python
import functools

import jax
import jax.numpy as jnp
from jax import lax
from jax.experimental import pallas as pl
from jax.experimental.pallas import tpu as pltpu
from jax.sharding import PartitionSpec as P

STEP = 0.3
EPS = 1e-06
F32 = jnp.float32
BF16 = jnp.bfloat16
PEERS = 16
WORD = 256
VMEM = pl.BlockSpec(memory_space=pltpu.VMEM)
HBM = pl.BlockSpec(memory_space=pltpu.HBM)


def call(body, outs, args, flops=1 << 22, specs=None, out_specs=None, scratch=(), aliases=None):
    moved = sum(a.size * a.dtype.itemsize for a in args)
    return pl.pallas_call(
        body,
        out_shape=[jax.ShapeDtypeStruct(shape, dtype) for shape, dtype in outs],
        in_specs=specs or [VMEM] * len(args),
        out_specs=out_specs or [VMEM] * len(outs),
        scratch_shapes=scratch,
        input_output_aliases=aliases or {},
        compiler_params=pltpu.CompilerParams(vmem_limit_bytes=32 << 20),
        cost_estimate=pl.CostEstimate(flops=flops, bytes_accessed=moved, transcendentals=0),
    )(*args)


def one_hot(ids, rows):
    grid = lax.broadcasted_iota(jnp.int16, (rows, ids.shape[1]), 0)
    return jnp.where(grid == ids.astype(jnp.int16), jnp.ones((), BF16), jnp.zeros((), BF16))


def mm(a, b):
    return lax.dot_general(a, b, (((1,), (0,)), ((), ())), preferred_element_type=F32)


def mm_t(a, b):
    return lax.dot_general(a, b, (((1,), (1,)), ((), ())), preferred_element_type=F32)


def core_of():
    return lax.axis_index("edge") & 1


def pieces(length):
    return [(at, min(WORD, length - at)) for at in range(0, length, WORD)]


def id_plan(edges, negatives):
    plan, row = [], 0
    for which, length, digits in ((0, edges, 2), (1, edges, 2), (2, edges, 1), (3, negatives, 1)):
        for digit in range(digits):
            plan.append((which, digit, row, length))
            row += len(pieces(length))
    return plan, -(-row // 32) * 32


def pack_kernel(block, src_ids, dst_ids, rel_ids, neg_ids, table, id_table, in_block, *scratch):
    held, sems, rows_f = scratch[:4], scratch[4], scratch[5]
    sources = (src_ids, dst_ids, rel_ids, neg_ids)
    copies = [pltpu.make_async_copy(block, in_block, sems.at[4])]
    for at, (source, target) in enumerate(zip(sources, held)):
        copies.append(pltpu.make_async_copy(source, target, sems.at[at]))
    for copy in copies:
        copy.start()
    for copy in copies[1:]:
        copy.wait()
    width = block.shape[0]
    plan, _ = id_plan(src_ids.shape[1], neg_ids.shape[1])
    rows_f[...] = jnp.full(rows_f.shape, -1.0, F32)
    for which, digit, row, length in plan:
        ids = held[which][...]
        ids = ids >> 8 if digit else ids & 255
        for step, (at, size) in enumerate(pieces(length)):
            rows_f[row + step : row + step + 1, :size] = ids[:, at : at + size].astype(F32)
    table[width:, :] = rows_f[...].astype(BF16)
    id_table[...] = rows_f[...].astype(BF16)
    copies[0].wait()
    table[:width, :] = in_block[...].astype(BF16)


def unpack(table, width, edges, negatives):
    plan, _ = id_plan(edges, negatives)
    rows_f = table[width:, :].astype(F32)
    out = [None] * 4
    for which, digit, row, length in plan:
        parts = [
            rows_f[row + step : row + step + 1, : -(-size // 128) * 128]
            for step, (_, size) in enumerate(pieces(length))
        ]
        ids = jnp.concatenate(parts, axis=1).astype(jnp.int32)
        out[which] = out[which] + ids * 256 if digit else ids
    return out


def counts(neg_at, rows):
    ones = jnp.ones((8, neg_at.shape[1]), BF16)
    return mm_t(ones, one_hot(neg_at, rows))[:1, :]


def gather_kernel(
    negatives,
    own,
    hot,
    rel,
    block_s,
    hot_s,
    rel_s,
    src_out,
    rel_out,
    dst_out,
    query_out,
    hot_bf,
    rel_bf,
    states,
):
    width, rows = hot.shape[0], own.shape[1]
    states[...] = jnp.zeros(states.shape, F32)
    src_at, dst_at, rel_at, neg_at = unpack(own, width, src_out.shape[1], negatives)
    states[4:5, :rows] = counts(neg_at, rows)
    for at, state in enumerate((block_s, hot_s, rel_s)):
        states[at : at + 1, : state.shape[1]] = state[...]
    hot_rows = hot.shape[1]
    hot_bf[...] = hot[...].astype(BF16)
    rel_bf[...] = rel[...].astype(BF16)
    src_out[...] = (
        mm(own[:width, :], one_hot(src_at, rows))
        + mm(hot_bf[...], one_hot(src_at - rows, hot_rows))
    ).astype(BF16)
    rel_out[...] = mm(rel_bf[...], one_hot(rel_at, rel.shape[1])).astype(BF16)
    query_out[...] = (src_out[...].astype(F32) * rel_out[...].astype(F32)).astype(BF16)
    dst_out[...] = mm(hot_bf[...], one_hot(dst_at - rows, hot_rows)).astype(BF16)


def far_kernel(negatives, ids, own, hot, rel, src_out, dst_out, rel_out, count_out):
    width, hot_rows = hot.shape
    rows = own.shape[1]
    src_at, dst_at, rel_at, neg_at = unpack(ids, 0, src_out.shape[1], negatives)
    ends = jnp.concatenate([src_at, dst_at], axis=1)
    from_hot = mm(hot[...], one_hot(ends - rows, hot_rows))
    edges = src_out.shape[1]
    src_out[...] = from_hot[:, :edges].astype(BF16)
    dst_out[...] = (mm(own[:width, :], one_hot(dst_at, rows)) + from_hot[:, edges:]).astype(BF16)
    rel_out[...] = mm(rel[...], one_hot(rel_at, rel.shape[1])).astype(BF16)
    count_out[...] = jnp.broadcast_to(counts(neg_at, rows), count_out.shape)


def edge_grads(partner, src, rel, dst, query, count):
    query_f = query.astype(F32)
    positive = jnp.sum(query_f * dst, axis=0, keepdims=True)
    pos_grad = -1.0 / (1.0 + jnp.exp(positive))
    scores = mm(partner.T, query)
    sig = (1.0 / (1.0 + jnp.exp(-scores))).astype(BF16)
    weighed = (partner.astype(F32) * count).astype(BF16)
    query_grad = pos_grad * dst + mm(weighed, sig)
    src_grad = (query_grad * rel).astype(BF16)
    kind_grad = (query_grad * src).astype(BF16)
    dst_grad = (pos_grad * query_f).astype(BF16)
    return sig, src_grad, kind_grad, dst_grad


def grad_kernel(
    negatives,
    own,
    partner,
    far_ids,
    far_src_hot,
    far_dst_rows,
    far_rel_rows,
    far_count,
    src,
    rel_rows,
    dst_hot,
    near_query,
    states,
    keep,
    send,
):
    width, edges = src.shape
    rows = own.shape[1]
    half = rows // 2
    side = lax.axis_index("bucket") // (lax.axis_size("bucket") // 2)
    own_table, partner_table = own[:width, :], partner[:width, :]

    def hot_hits(at):
        return one_hot(at - rows - side * rows, rows)

    near_src, near_dst, near_rel, _ = unpack(own, width, edges, negatives)
    dst = mm(partner_table, one_hot(near_dst, rows)) + dst_hot[...].astype(F32)
    _, near_src_grad, near_kind_grad, near_dst_grad = edge_grads(
        partner_table,
        src[...].astype(F32),
        rel_rows[...].astype(F32),
        dst,
        near_query[...],
        states[4:5, :rows],
    )
    far_src, far_dst, far_rel, _ = unpack(far_ids, 0, edges, negatives)
    src_rows = mm(partner_table, one_hot(far_src, rows)) + far_src_hot[...].astype(F32)
    dst_rows = far_dst_rows[...].astype(F32)
    kind_rows = far_rel_rows[...].astype(F32)
    query = (src_rows * kind_rows).astype(BF16)
    count = far_count[:1, :]
    sig, far_src_grad, far_kind_grad, far_dst_grad = edge_grads(
        own_table, src_rows, kind_rows, dst_rows, query, count
    )
    cold = jnp.concatenate([near_src_grad, far_dst_grad], axis=1)
    cold_at = jnp.concatenate([near_src, far_dst], axis=1)
    block_sum = mm_t(query, sig) * count + mm_t(cold, one_hot(cold_at, rows))
    named = jnp.concatenate([near_dst_grad, cold, far_src_grad], axis=1)
    named_at = jnp.concatenate([near_dst, cold_at, far_src], axis=1)
    hot_sum = mm_t(named, hot_hits(named_at))
    kind_grad = jnp.concatenate([near_kind_grad, far_kind_grad], axis=1)
    kind_at = jnp.concatenate([near_rel, far_rel], axis=1)
    kind_sum = mm_t(kind_grad, one_hot(kind_at - side * half, half))

    @pl.when(core_of() == 0)
    def _():
        keep[:, :rows] = block_sum
        keep[:, rows:] = hot_sum
        send[:, :half] = kind_sum.astype(BF16)
        send[:, half:rows] = jnp.zeros((width, half), BF16)
        send[:, rows:] = hot_sum.astype(BF16)

    @pl.when(core_of() == 1)
    def _():
        keep[:, :half] = kind_sum
        keep[:, half:rows] = jnp.zeros((width, half), F32)
        keep[:, rows:] = hot_sum
        send[:, :rows] = block_sum.astype(BF16)
        send[:, rows:] = hot_sum.astype(BF16)


SIDES = (range(PEERS // 2), range(PEERS // 2, PEERS))
LANES = 128


def cuts(width):
    whole = width // PEERS
    last = width // (4 * PEERS)
    return whole, whole - last, last


def slot_rows(width):
    whole, near, last = cuts(width)
    sizes = (
        (2 * whole + 2 * near, 2 * whole + 2 * last),
        (2 * near, 4 * last),
        (2 * whole + 4 * near, 4 * whole + 4 * last),
    )
    return [-(-max(pair) // 8) * 8 for pair in sizes]


def merge_kernel(keep, got, out, sums, packed):
    width = keep.shape[0]
    whole, near, last = cuts(width)
    split = PEERS * near
    hot = slice(2 * LANES, 4 * LANES)

    def put(block, value):
        sums[block] = value

    def blank(end):
        if end < packed.shape[1]:
            packed[:, end:, :] = jnp.zeros((PEERS, packed.shape[1] - end, LANES), F32)

    for block in range(2):
        at = slice(hot.start + block * LANES, hot.start + (block + 1) * LANES)
        put(2 + block, keep[:, at] + got[:, at].astype(F32))

    @pl.when(core_of() == 0)
    def _():
        for block in range(2):
            at = slice(block * LANES, (block + 1) * LANES)
            put(block, keep[:, at] + got[:, at].astype(F32))
            for peer in range(PEERS):
                low = 2 * whole + block * near
                packed[peer, low : low + near, :] = sums[2 + block, peer * near : (peer + 1) * near, :]
        blank(2 * whole + 2 * near)

    @pl.when(core_of() == 1)
    def _():
        put(0, got[:, :LANES].astype(F32))
        put(1, keep[:, :LANES])
        for block in range(2):
            for peer in range(PEERS):
                low, start = 2 * whole + block * last, split + peer * last
                packed[peer, low : low + last, :] = sums[2 + block, start : start + last, :]
        blank(2 * whole + 2 * last)

    for block in range(2):
        for peer in range(PEERS):
            low = block * whole
            packed[peer, low : low + whole, :] = sums[block, peer * whole : (peer + 1) * whole, :]
    out[...] = packed[...].astype(BF16)


def peer_sum(ref, peers):
    total = ref[peers[0]].astype(F32)
    for peer in peers[1:]:
        total = total + ref[peer].astype(F32)
    return total


def first_kernel(width, got, out, held, total, row):
    whole, near, last = cuts(width)
    held[...] = jnp.zeros(held.shape, F32)
    row[...] = jnp.zeros(row.shape, F32)

    @pl.when(core_of() == 0)
    def _():
        total[...] = peer_sum(got, range(PEERS))
        held[: 2 * whole, :] = total[: 2 * whole, :]
        row[: 2 * near, :] = total[2 * whole : 2 * whole + 2 * near, :]

    @pl.when(core_of() == 1)
    def _():
        for side, peers in enumerate(SIDES):
            total[...] = peer_sum(got, peers)
            for core in range(2):
                at = (2 * core + side) * whole
                held[at : at + whole, :] = total[core * whole : (core + 1) * whole, :]
            at = side * 2 * last
            row[at : at + 2 * last, :] = total[2 * whole : 2 * whole + 2 * last, :]

    value = row[...].astype(BF16)
    for peer in range(PEERS):
        out[peer] = value


def second_kernel(width, got, held, out, total, row):
    whole, near, last = cuts(width)
    row[...] = jnp.zeros(row.shape, F32)

    @pl.when(core_of() == 0)
    def _():
        row[: 2 * whole, :] = held[: 2 * whole, :]
        for side, peers in enumerate(SIDES):
            total[...] = peer_sum(got, peers)
            at = 2 * whole + side * 2 * near
            row[at : at + 2 * near, :] = total[: 2 * near, :]

    @pl.when(core_of() == 1)
    def _():
        total[...] = peer_sum(got, range(PEERS))
        row[: 4 * whole, :] = held[: 4 * whole, :]
        row[4 * whole : 4 * whole + 4 * last, :] = total[: 4 * last, :]

    value = row[...].astype(BF16)
    for peer in range(PEERS):
        out[peer] = value


def stepped(table, column, grads, weights, states, held, state_held):
    at = slice(column * LANES, (column + 1) * LANES)
    total = jnp.sum(grads * grads, axis=0, keepdims=True) / grads.shape[0]
    total = states[table : table + 1, at] + total
    state_held[table : table + 1, at] = total
    held[:, at] = weights[:, at] - grads * (STEP / (jnp.sqrt(total) + EPS))


def written(table, held, state_held, out, state_out, sems):
    state = state_held.at[table : table + 1, : held.shape[1]]
    copies = [
        pltpu.make_async_copy(held, out, sems.at[2 * table]),
        pltpu.make_async_copy(state, state_out, sems.at[2 * table + 1]),
    ]
    for copy in copies:
        copy.start()
    return copies


def near_hot(rows_f, hot_rows, whole, near):
    for column in range(hot_rows.shape[0]):
        for peer in range(PEERS):
            low = 2 * whole + column * near
            hot_rows[column, peer * near : (peer + 1) * near, :] = rows_f[peer, low : low + near, :]


def last_hot(rows_f, hot_rows, whole, near, last):
    for column in range(hot_rows.shape[0]):
        for peer in range(PEERS):
            low, start = 4 * whole + column * last, PEERS * near + peer * last
            hot_rows[column, start : start + last, :] = rows_f[peer, low : low + last, :]


def whole_rows(rows_f, grads, whole, low):
    for peer in range(PEERS):
        grads[peer * whole : (peer + 1) * whole, :] = rows_f[peer, low : low + whole, :]
    return grads[...]


def early_kernel(
    mine, states, block, rel, new_b, new_bs, new_r, new_rs, hot_rows, rows_f, held, state_held, grads, sems
):
    whole, near, last = cuts(block.shape[0])
    rows_f[...] = mine[...].astype(F32)

    @pl.when(core_of() == 0)
    def _():
        for column in range(2):
            value = whole_rows(rows_f, grads, whole, column * whole)
            stepped(0, column, value, block, states, held, state_held)
        copies = written(0, held, state_held, new_b, new_bs, sems)
        near_hot(rows_f, hot_rows, whole, near)
        for copy in copies:
            copy.wait()

    @pl.when(core_of() == 1)
    def _():
        for column in range(2):
            value = whole_rows(rows_f, grads, whole, (2 + column) * whole)
            stepped(2, column, value, rel, states, held, state_held)
        copies = written(2, held, state_held, new_r, new_rs, sems)
        last_hot(rows_f, hot_rows, whole, near, last)
        for copy in copies:
            copy.wait()


def late_kernel(
    other, states, block, hot, rel, part, in_b, in_bs, in_r, in_rs, new_b, new_bs, new_r, new_rs, new_h, new_hs, *refs
):
    del in_b, in_bs, in_r, in_rs
    rows_f, hot_rows, held_hot, held, state_held, grads, sems = refs
    width = block.shape[0]
    whole, near, last = cuts(width)
    split = PEERS * near
    rows_f[...] = other[...].astype(F32)

    def hot_steps():
        for column in range(hot_rows.shape[0]):
            stepped(1, column, hot_rows[column], hot, states, held_hot, state_held)
        return written(1, held_hot, state_held, new_h, new_hs, sems)

    @pl.when(core_of() == 0)
    def _():
        hot_rows[:, :split, :] = part[:, :split, :]
        last_hot(rows_f, hot_rows, whole, near, last)
        copies = hot_steps()
        for column in range(2):
            value = whole_rows(rows_f, grads, whole, column * whole)
            stepped(2, column, value, rel, states, held, state_held)
        for copy in copies + written(2, held, state_held, new_r, new_rs, sems):
            copy.wait()

    @pl.when(core_of() == 1)
    def _():
        hot_rows[:, split:, :] = part[:, split:, :]
        near_hot(rows_f, hot_rows, whole, near)
        copies = hot_steps()
        for column in range(2):
            value = whole_rows(rows_f, grads, whole, column * whole)
            stepped(0, column, value, block, states, held, state_held)
        for copy in copies + written(0, held, state_held, new_b, new_bs, sems):
            copy.wait()


def flipped(x, axis, bit):
    return lax.ppermute(x, axis, [(i, i ^ bit) for i in range(lax.axis_size(axis))])


def exchanged(x, groups):
    return lax.all_to_all(x, ("bucket", "edge"), 0, 0, tiled=True, axis_index_groups=groups)


def edge_groups(core):
    n = lax.axis_size("edge")
    return [[b * n + e for e in range(core, n, 2)] for b in range(lax.axis_size("bucket"))]


def bucket_groups(core):
    n = lax.axis_size("edge")
    return [[b * n + e for b in range(lax.axis_size("bucket"))] for e in range(core, n, 2)]


def local(
    entity_block,
    block_state,
    hot_entities,
    hot_state,
    relations,
    relation_state,
    source_ids,
    target_ids,
    relation_ids,
    negative_ids,
):
    rows, width = entity_block.shape
    hot_rows = hot_entities.shape[0]
    edges = source_ids.shape[1]
    block_t, hot_t, rel_t = entity_block.T, hot_entities.T, relations.T
    negatives = negative_ids.shape[-1]
    ids = (source_ids, target_ids, relation_ids, negative_ids.reshape(1, -1))
    _, id_height = id_plan(edges, negatives)
    own, id_table = call(
        pack_kernel,
        [((width + id_height, rows), BF16), ((id_height, rows), BF16)],
        [pltpu.with_memory_space_constraint(part, pltpu.HBM) for part in (block_t, *ids)],
        specs=[HBM] * 5,
        scratch=[pltpu.VMEM((width, rows), F32)]
        + [pltpu.VMEM(part.shape, jnp.int32) for part in ids]
        + [pltpu.SemaphoreType.DMA((5,)), pltpu.VMEM((id_height, rows), F32)],
    )
    partner = flipped(own, "bucket", lax.axis_size("bucket") // 2)
    far_ids = flipped(id_table, "bucket", lax.axis_size("bucket") // 2)
    state_rows = [state.reshape(1, -1) for state in (block_state, hot_state, relation_state)]
    src, rel_rows, dst_hot, near_query, hot_bf, rel_bf, states = call(
        functools.partial(gather_kernel, negatives),
        [((width, edges), BF16)] * 4
        + [((width, hot_rows), BF16), ((width, rows), BF16), ((8, hot_rows), F32)],
        (own, hot_t, rel_t, *state_rows),
        1 << 30,
    )
    far = call(
        functools.partial(far_kernel, negatives),
        [((width, edges), BF16)] * 3 + [((8, rows), F32)],
        (far_ids, own, hot_bf, rel_bf),
        1 << 30,
    )
    keep, send = call(
        functools.partial(grad_kernel, negatives),
        [((width, 2 * rows), F32), ((width, 2 * rows), BF16)],
        (own, partner, far_ids, *far, src, rel_rows, dst_hot, near_query, states),
        1 << 31,
    )
    both = edge_groups(0) + bucket_groups(1)
    sizes = slot_rows(width)
    whole = width // PEERS
    slots = [((PEERS, size, LANES), BF16) for size in sizes]
    rows_f = [pltpu.VMEM((size, LANES), F32) for size in sizes]
    (mixed,) = call(
        merge_kernel,
        [slots[0]],
        (keep, flipped(send, "edge", 1)),
        scratch=[pltpu.VMEM((4, width, LANES), F32), pltpu.VMEM((PEERS, sizes[0], LANES), F32)],
    )
    mixed = exchanged(mixed, both)
    hot_part, held = call(
        functools.partial(first_kernel, width),
        [slots[1], ((-(-4 * whole // 8) * 8, LANES), F32)],
        (mixed,),
        scratch=[rows_f[0], rows_f[1]],
    )
    hot_part = exchanged(hot_part, bucket_groups(0) + edge_groups(1))
    (totals,) = call(
        functools.partial(second_kernel, width),
        [slots[2]],
        (hot_part, held),
        scratch=[rows_f[1], rows_f[2]],
    )
    mine = exchanged(totals, both)
    other = flipped(mine, "edge", 1)
    block_s, hot_s, rel_s = [(part.shape, F32) for part in state_rows]
    block_like, hot_like = (block_t.shape, F32), (hot_t.shape, F32)
    columns = ((hot_rows // LANES, width, LANES), F32)
    held = [pltpu.VMEM(block_t.shape, F32), pltpu.VMEM(states.shape, F32)]
    held += [pltpu.VMEM((width, LANES), F32), pltpu.SemaphoreType.DMA((6,))]
    *done, part = call(
        early_kernel,
        [block_like, block_s, block_like, rel_s, columns],
        (mine, states, block_t, rel_t),
        out_specs=[HBM] * 4 + [VMEM],
        scratch=[pltpu.VMEM(mine.shape, F32)] + held,
    )
    new_block, new_block_state, new_relations, new_relation_state, new_hot, new_hot_state = call(
        late_kernel,
        [block_like, block_s, block_like, rel_s, hot_like, hot_s],
        (other, states, block_t, hot_t, rel_t, part, *done),
        specs=[VMEM] * 6 + [HBM] * 4,
        out_specs=[HBM] * 6,
        scratch=[pltpu.VMEM(mine.shape, F32), pltpu.VMEM(*columns), pltpu.VMEM(*hot_like)] + held,
        aliases={6 + at: at for at in range(4)},
    )
    new_block_state, new_hot_state, new_relation_state = [
        part.reshape(-1) for part in (new_block_state, new_hot_state, new_relation_state)
    ]
    return (
        new_block.T,
        new_block_state,
        new_hot.T,
        new_hot_state,
        new_relations.T,
        new_relation_state,
    )


def solution(mesh):
    placed = (
        P("bucket", None),
        P("bucket"),
        P(),
        P(),
        P("edge", None),
        P("edge"),
        P("bucket", "edge"),
        P("bucket", "edge"),
        P("bucket", "edge"),
        P("bucket", "edge", None),
    )
    return jax.shard_map(
        local,
        mesh=mesh,
        in_specs=placed,
        out_specs=(P("bucket", None), P("bucket"), P(), P(), P("edge", None), P("edge")),
        check_vma=False,
    )
```

```python
import functools

import jax
import jax.numpy as jnp
from jax import lax
from jax.experimental import pallas as pl
from jax.experimental.pallas import tpu as pltpu
from jax.sharding import PartitionSpec as P

STEP = 0.3
EPS = 1e-06
F32 = jnp.float32
BF16 = jnp.bfloat16
PEERS = 16
WORD = 256
VMEM = pl.BlockSpec(memory_space=pltpu.VMEM)
HBM = pl.BlockSpec(memory_space=pltpu.HBM)


def call(body, outs, args, flops=1 << 22, specs=None, out_specs=None, scratch=(), aliases=None):
    moved = sum(a.size * a.dtype.itemsize for a in args)
    return pl.pallas_call(
        body,
        out_shape=[jax.ShapeDtypeStruct(shape, dtype) for shape, dtype in outs],
        in_specs=specs or [VMEM] * len(args),
        out_specs=out_specs or [VMEM] * len(outs),
        scratch_shapes=scratch,
        input_output_aliases=aliases or {},
        compiler_params=pltpu.CompilerParams(vmem_limit_bytes=32 << 20),
        cost_estimate=pl.CostEstimate(flops=flops, bytes_accessed=moved, transcendentals=0),
    )(*args)


def one_hot(ids, rows):
    grid = lax.broadcasted_iota(jnp.int16, (rows, ids.shape[1]), 0)
    return jnp.where(grid == ids.astype(jnp.int16), jnp.ones((), BF16), jnp.zeros((), BF16))


def mm(a, b):
    return lax.dot_general(a, b, (((1,), (0,)), ((), ())), preferred_element_type=F32)


def mm_t(a, b):
    return lax.dot_general(a, b, (((1,), (1,)), ((), ())), preferred_element_type=F32)


def core_of():
    return lax.axis_index("edge") & 1


def pieces(length):
    return [(at, min(WORD, length - at)) for at in range(0, length, WORD)]


def id_plan(edges, negatives):
    plan, row = [], 0
    for which, length, digits in ((0, edges, 2), (1, edges, 2), (2, edges, 1), (3, negatives, 1)):
        for digit in range(digits):
            plan.append((which, digit, row, length))
            row += len(pieces(length))
    return plan, -(-row // 32) * 32


def pack_kernel(block, src_ids, dst_ids, rel_ids, neg_ids, table, in_block, *scratch):
    held, sems, rows_f = scratch[:4], scratch[4], scratch[5]
    sources = (src_ids, dst_ids, rel_ids, neg_ids)
    copies = [pltpu.make_async_copy(block, in_block, sems.at[4])]
    for at, (source, target) in enumerate(zip(sources, held)):
        copies.append(pltpu.make_async_copy(source, target, sems.at[at]))
    for copy in copies:
        copy.start()
    for copy in copies[1:]:
        copy.wait()
    width = block.shape[0]
    plan, _ = id_plan(src_ids.shape[1], neg_ids.shape[1])
    rows_f[...] = jnp.full(rows_f.shape, -1.0, F32)
    for which, digit, row, length in plan:
        ids = held[which][...]
        ids = ids >> 8 if digit else ids & 255
        for step, (at, size) in enumerate(pieces(length)):
            rows_f[row + step : row + step + 1, :size] = ids[:, at : at + size].astype(F32)
    table[width:, :] = rows_f[...].astype(BF16)
    copies[0].wait()
    table[:width, :] = in_block[...].astype(BF16)


def unpack(table, width, edges, negatives):
    plan, _ = id_plan(edges, negatives)
    rows_f = table[width:, :].astype(F32)
    out = [None] * 4
    for which, digit, row, length in plan:
        parts = [
            rows_f[row + step : row + step + 1, : -(-size // 128) * 128]
            for step, (_, size) in enumerate(pieces(length))
        ]
        ids = jnp.concatenate(parts, axis=1).astype(jnp.int32)
        out[which] = out[which] + ids * 256 if digit else ids
    return out


def counts(neg_at, rows):
    ones = jnp.ones((8, neg_at.shape[1]), BF16)
    return mm_t(ones, one_hot(neg_at, rows))[:1, :]


def gather_kernel(
    negatives,
    own,
    hot,
    rel,
    block_s,
    hot_s,
    rel_s,
    src_out,
    rel_out,
    dst_out,
    query_out,
    hot_bf,
    rel_bf,
    states,
):
    width, rows = hot.shape[0], own.shape[1]
    states[...] = jnp.zeros(states.shape, F32)
    src_at, dst_at, rel_at, neg_at = unpack(own, width, src_out.shape[1], negatives)
    states[4:5, :rows] = counts(neg_at, rows)
    for at, state in enumerate((block_s, hot_s, rel_s)):
        states[at : at + 1, : state.shape[1]] = state[...]
    hot_rows = hot.shape[1]
    hot_bf[...] = hot[...].astype(BF16)
    rel_bf[...] = rel[...].astype(BF16)
    src_out[...] = (
        mm(own[:width, :], one_hot(src_at, rows))
        + mm(hot_bf[...], one_hot(src_at - rows, hot_rows))
    ).astype(BF16)
    rel_out[...] = mm(rel_bf[...], one_hot(rel_at, rel.shape[1])).astype(BF16)
    query_out[...] = (src_out[...].astype(F32) * rel_out[...].astype(F32)).astype(BF16)
    dst_out[...] = mm(hot_bf[...], one_hot(dst_at - rows, hot_rows)).astype(BF16)


def edge_grads(partner, src, rel, dst, query, count):
    query_f = query.astype(F32)
    positive = jnp.sum(query_f * dst, axis=0, keepdims=True)
    pos_grad = -1.0 / (1.0 + jnp.exp(positive))
    scores = mm(partner.T, query)
    sig = (1.0 / (1.0 + jnp.exp(-scores))).astype(BF16)
    weighed = (partner.astype(F32) * count).astype(BF16)
    query_grad = pos_grad * dst + mm(weighed, sig)
    src_grad = (query_grad * rel).astype(BF16)
    kind_grad = (query_grad * src).astype(BF16)
    dst_grad = (pos_grad * query_f).astype(BF16)
    return sig, src_grad, kind_grad, dst_grad


def grad_kernel(
    negatives, own, partner, hot, rel, src, rel_rows, dst_hot, near_query, states, keep, send
):
    width, edges = src.shape
    rows, hot_rows = own.shape[1], hot.shape[1]
    half = rows // 2
    side = lax.axis_index("bucket") // (lax.axis_size("bucket") // 2)
    own_table, partner_table = own[:width, :], partner[:width, :]

    def hot_hits(at):
        return one_hot(at - rows - side * rows, rows)

    near_src, near_dst, near_rel, _ = unpack(own, width, edges, negatives)
    dst = mm(partner_table, one_hot(near_dst, rows)) + dst_hot[...].astype(F32)
    _, near_src_grad, near_kind_grad, near_dst_grad = edge_grads(
        partner_table,
        src[...].astype(F32),
        rel_rows[...].astype(F32),
        dst,
        near_query[...],
        states[4:5, :rows],
    )
    far_src, far_dst, far_rel, far_neg = unpack(partner, width, edges, negatives)
    ends = jnp.concatenate([far_src, far_dst], axis=1)
    from_hot = mm(hot[...], one_hot(ends - rows, hot_rows))
    src_rows = mm(partner_table, one_hot(far_src, rows)) + from_hot[:, :edges]
    dst_rows = mm(own_table, one_hot(far_dst, rows)) + from_hot[:, edges:]
    kind_rows = mm(rel[...], one_hot(far_rel, rel.shape[1]))
    query = (src_rows * kind_rows).astype(BF16)
    count = counts(far_neg, rows)
    sig, far_src_grad, far_kind_grad, far_dst_grad = edge_grads(
        own_table, src_rows, kind_rows, dst_rows, query, count
    )
    cold = jnp.concatenate([near_src_grad, far_dst_grad], axis=1)
    cold_at = jnp.concatenate([near_src, far_dst], axis=1)
    block_sum = mm_t(query, sig) * count + mm_t(cold, one_hot(cold_at, rows))
    named = jnp.concatenate([near_dst_grad, cold, far_src_grad], axis=1)
    named_at = jnp.concatenate([near_dst, cold_at, far_src], axis=1)
    hot_sum = mm_t(named, hot_hits(named_at))
    kind_grad = jnp.concatenate([near_kind_grad, far_kind_grad], axis=1)
    kind_at = jnp.concatenate([near_rel, far_rel], axis=1)
    kind_sum = mm_t(kind_grad, one_hot(kind_at - side * half, half))

    split = PEERS * cuts(width)[1]

    @pl.when(core_of() == 0)
    def _():
        keep[:, :rows] = block_sum
        keep[:, rows:] = hot_sum
        send[:width, :half] = kind_sum.astype(BF16)
        send[:width, half:] = jnp.zeros((width, half), BF16)
        send[width : 2 * width - split, :] = hot_sum[split:, :].astype(BF16)
        send[2 * width - split :, :] = jnp.zeros((2 * split - width, rows), BF16)

    @pl.when(core_of() == 1)
    def _():
        keep[:, :half] = kind_sum
        keep[:, half:rows] = jnp.zeros((width, half), F32)
        keep[:, rows:] = hot_sum
        send[:width, :] = block_sum.astype(BF16)
        send[width:, :] = hot_sum[:split, :].astype(BF16)


SIDES = (range(PEERS // 2), range(PEERS // 2, PEERS))
LANES = 128


def cuts(width):
    whole = width // PEERS
    last = width // (4 * PEERS)
    return whole, whole - last, last


def slot_rows(width):
    whole, near, last = cuts(width)
    sizes = (
        (2 * whole + 2 * near, 2 * whole + 2 * last),
        (2 * near, 4 * last),
        (2 * whole + 4 * near, 4 * whole + 4 * last),
    )
    return [-(-max(pair) // 8) * 8 for pair in sizes]


def merge_kernel(keep, got, out, sums, packed):
    width = keep.shape[0]
    whole, near, last = cuts(width)
    split = PEERS * near
    hot = slice(2 * LANES, 4 * LANES)

    def put(block, value):
        sums[block] = value

    def blank(end):
        if end < packed.shape[1]:
            packed[:, end:, :] = jnp.zeros((PEERS, packed.shape[1] - end, LANES), F32)

    def put_hot(low, high):
        for block in range(2):
            at = slice(hot.start + block * LANES, hot.start + (block + 1) * LANES)
            came = got[width : width + high - low, block * LANES : (block + 1) * LANES]
            sums[2 + block, low:high, :] = keep[low:high, at] + came.astype(F32)

    @pl.when(core_of() == 0)
    def _():
        put_hot(0, split)
        for block in range(2):
            at = slice(block * LANES, (block + 1) * LANES)
            put(block, keep[:, at] + got[:width, at].astype(F32))
            for peer in range(PEERS):
                low = 2 * whole + block * near
                packed[peer, low : low + near, :] = sums[2 + block, peer * near : (peer + 1) * near, :]
        blank(2 * whole + 2 * near)

    @pl.when(core_of() == 1)
    def _():
        put_hot(split, width)
        put(0, got[:width, :LANES].astype(F32))
        put(1, keep[:, :LANES])
        for block in range(2):
            for peer in range(PEERS):
                low, start = 2 * whole + block * last, split + peer * last
                packed[peer, low : low + last, :] = sums[2 + block, start : start + last, :]
        blank(2 * whole + 2 * last)

    for block in range(2):
        for peer in range(PEERS):
            low = block * whole
            packed[peer, low : low + whole, :] = sums[block, peer * whole : (peer + 1) * whole, :]
    out[...] = packed[...].astype(BF16)


def peer_sum(ref, peers):
    total = ref[peers[0]].astype(F32)
    for peer in peers[1:]:
        total = total + ref[peer].astype(F32)
    return total


def first_kernel(width, got, out, held, total, row):
    whole, near, last = cuts(width)
    held[...] = jnp.zeros(held.shape, F32)
    row[...] = jnp.zeros(row.shape, F32)

    @pl.when(core_of() == 0)
    def _():
        total[...] = peer_sum(got, range(PEERS))
        held[: 2 * whole, :] = total[: 2 * whole, :]
        row[: 2 * near, :] = total[2 * whole : 2 * whole + 2 * near, :]

    @pl.when(core_of() == 1)
    def _():
        for side, peers in enumerate(SIDES):
            total[...] = peer_sum(got, peers)
            for core in range(2):
                at = (2 * core + side) * whole
                held[at : at + whole, :] = total[core * whole : (core + 1) * whole, :]
            at = side * 2 * last
            row[at : at + 2 * last, :] = total[2 * whole : 2 * whole + 2 * last, :]

    value = row[...].astype(BF16)
    for peer in range(PEERS):
        out[peer] = value


def second_kernel(width, got, held, out, total, row):
    whole, near, last = cuts(width)
    row[...] = jnp.zeros(row.shape, F32)

    @pl.when(core_of() == 0)
    def _():
        row[: 2 * whole, :] = held[: 2 * whole, :]
        for side, peers in enumerate(SIDES):
            total[...] = peer_sum(got, peers)
            at = 2 * whole + side * 2 * near
            row[at : at + 2 * near, :] = total[: 2 * near, :]

    @pl.when(core_of() == 1)
    def _():
        total[...] = peer_sum(got, range(PEERS))
        row[: 4 * whole, :] = held[: 4 * whole, :]
        row[4 * whole : 4 * whole + 4 * last, :] = total[: 4 * last, :]

    value = row[...].astype(BF16)
    for peer in range(PEERS):
        out[peer] = value


def stepped(table, column, grads, weights, states, held, state_held):
    at = slice(column * LANES, (column + 1) * LANES)
    total = jnp.sum(grads * grads, axis=0, keepdims=True) / grads.shape[0]
    total = states[table : table + 1, at] + total
    state_held[table : table + 1, at] = total
    held[:, at] = weights[:, at] - grads * (STEP / (jnp.sqrt(total) + EPS))


def written(table, held, state_held, out, state_out, sems):
    state = state_held.at[table : table + 1, : held.shape[1]]
    copies = [
        pltpu.make_async_copy(held, out, sems.at[2 * table]),
        pltpu.make_async_copy(state, state_out, sems.at[2 * table + 1]),
    ]
    for copy in copies:
        copy.start()
    return copies


def near_hot(rows_f, hot_rows, whole, near):
    for column in range(hot_rows.shape[0]):
        for peer in range(PEERS):
            low = 2 * whole + column * near
            hot_rows[column, peer * near : (peer + 1) * near, :] = rows_f[peer, low : low + near, :]


def last_hot(rows_f, hot_rows, whole, near, last):
    for column in range(hot_rows.shape[0]):
        for peer in range(PEERS):
            low, start = 4 * whole + column * last, PEERS * near + peer * last
            hot_rows[column, start : start + last, :] = rows_f[peer, low : low + last, :]


def whole_rows(rows_f, grads, whole, low):
    for peer in range(PEERS):
        grads[peer * whole : (peer + 1) * whole, :] = rows_f[peer, low : low + whole, :]
    return grads[...]


def early_kernel(
    mine, states, block, rel, new_b, new_bs, new_r, new_rs, hot_rows, rows_f, held, state_held, grads, sems
):
    whole, near, last = cuts(block.shape[0])
    rows_f[...] = mine[...].astype(F32)

    @pl.when(core_of() == 0)
    def _():
        for column in range(2):
            value = whole_rows(rows_f, grads, whole, column * whole)
            stepped(0, column, value, block, states, held, state_held)
        copies = written(0, held, state_held, new_b, new_bs, sems)
        near_hot(rows_f, hot_rows, whole, near)
        for copy in copies:
            copy.wait()

    @pl.when(core_of() == 1)
    def _():
        for column in range(2):
            value = whole_rows(rows_f, grads, whole, (2 + column) * whole)
            stepped(2, column, value, rel, states, held, state_held)
        copies = written(2, held, state_held, new_r, new_rs, sems)
        last_hot(rows_f, hot_rows, whole, near, last)
        for copy in copies:
            copy.wait()


def late_kernel(
    other, states, block, hot, rel, part, in_b, in_bs, in_r, in_rs, new_b, new_bs, new_r, new_rs, new_h, new_hs, *refs
):
    del in_b, in_bs, in_r, in_rs
    rows_f, hot_rows, held_hot, held, state_held, grads, sems = refs
    width = block.shape[0]
    whole, near, last = cuts(width)
    split = PEERS * near
    rows_f[...] = other[...].astype(F32)

    def hot_steps():
        for column in range(hot_rows.shape[0]):
            stepped(1, column, hot_rows[column], hot, states, held_hot, state_held)
        return written(1, held_hot, state_held, new_h, new_hs, sems)

    @pl.when(core_of() == 0)
    def _():
        hot_rows[:, :split, :] = part[:, :split, :]
        last_hot(rows_f, hot_rows, whole, near, last)
        copies = hot_steps()
        for column in range(2):
            value = whole_rows(rows_f, grads, whole, column * whole)
            stepped(2, column, value, rel, states, held, state_held)
        for copy in copies + written(2, held, state_held, new_r, new_rs, sems):
            copy.wait()

    @pl.when(core_of() == 1)
    def _():
        hot_rows[:, split:, :] = part[:, split:, :]
        near_hot(rows_f, hot_rows, whole, near)
        copies = hot_steps()
        for column in range(2):
            value = whole_rows(rows_f, grads, whole, column * whole)
            stepped(0, column, value, block, states, held, state_held)
        for copy in copies + written(0, held, state_held, new_b, new_bs, sems):
            copy.wait()


def flipped(x, axis, bit):
    return lax.ppermute(x, axis, [(i, i ^ bit) for i in range(lax.axis_size(axis))])


def exchanged(x, groups):
    return lax.all_to_all(x, ("bucket", "edge"), 0, 0, tiled=True, axis_index_groups=groups)


def edge_groups(core):
    n = lax.axis_size("edge")
    return [[b * n + e for e in range(core, n, 2)] for b in range(lax.axis_size("bucket"))]


def bucket_groups(core):
    n = lax.axis_size("edge")
    return [[b * n + e for b in range(lax.axis_size("bucket"))] for e in range(core, n, 2)]


def local(
    entity_block,
    block_state,
    hot_entities,
    hot_state,
    relations,
    relation_state,
    source_ids,
    target_ids,
    relation_ids,
    negative_ids,
):
    rows, width = entity_block.shape
    hot_rows = hot_entities.shape[0]
    edges = source_ids.shape[1]
    block_t, hot_t, rel_t = entity_block.T, hot_entities.T, relations.T
    negatives = negative_ids.shape[-1]
    ids = (source_ids, target_ids, relation_ids, negative_ids.reshape(1, -1))
    _, id_height = id_plan(edges, negatives)
    (own,) = call(
        pack_kernel,
        [((width + id_height, rows), BF16)],
        [pltpu.with_memory_space_constraint(part, pltpu.HBM) for part in (block_t, *ids)],
        specs=[HBM] * 5,
        scratch=[pltpu.VMEM((width, rows), F32)]
        + [pltpu.VMEM(part.shape, jnp.int32) for part in ids]
        + [pltpu.SemaphoreType.DMA((5,)), pltpu.VMEM((id_height, rows), F32)],
    )
    partner = flipped(own, "bucket", lax.axis_size("bucket") // 2)
    state_rows = [state.reshape(1, -1) for state in (block_state, hot_state, relation_state)]
    src, rel_rows, dst_hot, near_query, hot_bf, rel_bf, states = call(
        functools.partial(gather_kernel, negatives),
        [((width, edges), BF16)] * 4
        + [((width, hot_rows), BF16), ((width, rows), BF16), ((8, hot_rows), F32)],
        (own, hot_t, rel_t, *state_rows),
        1 << 30,
    )
    keep, send = call(
        functools.partial(grad_kernel, negatives),
        [((width, 2 * rows), F32), ((width + PEERS * cuts(width)[1], rows), BF16)],
        (own, partner, hot_bf, rel_bf, src, rel_rows, dst_hot, near_query, states),
        1 << 31,
    )
    both = edge_groups(0) + bucket_groups(1)
    sizes = slot_rows(width)
    whole = width // PEERS
    slots = [((PEERS, size, LANES), BF16) for size in sizes]
    rows_f = [pltpu.VMEM((size, LANES), F32) for size in sizes]
    (mixed,) = call(
        merge_kernel,
        [slots[0]],
        (keep, flipped(send, "edge", 1)),
        scratch=[pltpu.VMEM((4, width, LANES), F32), pltpu.VMEM((PEERS, sizes[0], LANES), F32)],
    )
    mixed = exchanged(mixed, both)
    hot_part, held = call(
        functools.partial(first_kernel, width),
        [slots[1], ((-(-4 * whole // 8) * 8, LANES), F32)],
        (mixed,),
        scratch=[rows_f[0], rows_f[1]],
    )
    hot_part = exchanged(hot_part, bucket_groups(0) + edge_groups(1))
    (totals,) = call(
        functools.partial(second_kernel, width),
        [slots[2]],
        (hot_part, held),
        scratch=[rows_f[1], rows_f[2]],
    )
    mine = exchanged(totals, both)
    other = flipped(mine, "edge", 1)
    block_s, hot_s, rel_s = [(part.shape, F32) for part in state_rows]
    block_like, hot_like = (block_t.shape, F32), (hot_t.shape, F32)
    columns = ((hot_rows // LANES, width, LANES), F32)
    held = [pltpu.VMEM(block_t.shape, F32), pltpu.VMEM(states.shape, F32)]
    held += [pltpu.VMEM((width, LANES), F32), pltpu.SemaphoreType.DMA((6,))]
    *done, part = call(
        early_kernel,
        [block_like, block_s, block_like, rel_s, columns],
        (mine, states, block_t, rel_t),
        out_specs=[HBM] * 4 + [VMEM],
        scratch=[pltpu.VMEM(mine.shape, F32)] + held,
    )
    new_block, new_block_state, new_relations, new_relation_state, new_hot, new_hot_state = call(
        late_kernel,
        [block_like, block_s, block_like, rel_s, hot_like, hot_s],
        (other, states, block_t, hot_t, rel_t, part, *done),
        specs=[VMEM] * 6 + [HBM] * 4,
        out_specs=[HBM] * 6,
        scratch=[pltpu.VMEM(mine.shape, F32), pltpu.VMEM(*columns), pltpu.VMEM(*hot_like)] + held,
        aliases={6 + at: at for at in range(4)},
    )
    new_block_state, new_hot_state, new_relation_state = [
        part.reshape(-1) for part in (new_block_state, new_hot_state, new_relation_state)
    ]
    return (
        new_block.T,
        new_block_state,
        new_hot.T,
        new_hot_state,
        new_relations.T,
        new_relation_state,
    )


def solution(mesh):
    placed = (
        P("bucket", None),
        P("bucket"),
        P(),
        P(),
        P("edge", None),
        P("edge"),
        P("bucket", "edge"),
        P("bucket", "edge"),
        P("bucket", "edge"),
        P("bucket", "edge", None),
    )
    return jax.shard_map(
        local,
        mesh=mesh,
        in_specs=placed,
        out_specs=(P("bucket", None), P("bucket"), P(), P(), P("edge", None), P("edge")),
        check_vma=False,
    )
```
